32 devices in a mesh: epoch: 8 (over z, y), col: 4 (over x, core).
Axes of the slice: x: 2, y: 2, z: 4, core: 2. Of those that a mesh axis runs over, the one named last changes fastest.
Arguments:
- partials: bfloat16 [2048, 8192], P('epoch', 'col'), may hold values from -6 to 6
- gaps: int32 [2048], P('epoch'), may hold values 0 or 1
- arc_start: int32 [1], replicated, may hold values from 512 to 1535
- taps: bfloat16 [241], replicated, may hold values from -0.375 to 0.375
Outputs:
- normal_matrix: float32 [8192, 8192], P('col', 'epoch')
The draws below stay inside these ranges and needn't reach their ends.
All inputs are finite; a program needn't handle non-finite values. No bound on the sum of `gaps` on one device may be relied on, other than what follows from the above.
Results may differ from the reference program's by a relative error of at most 0.0026.
Values may be sent and summed in bfloat16 or wider, within the bound.
A program may use at most 64 MiB of HBM per device.

```python
import jax
import jax.numpy as jnp
from jax import lax

P_SIZE = 8192
TAPS = 241
E_DEV = 256
EPOCHS = 2048


def plant(drawn, key, least, largest):
    extent = drawn.shape
    place = [jax.random.randint(jax.random.fold_in(key, axis), (), 0, extent[axis]) for axis in range(len(extent))]
    drawn = drawn.at[tuple(place)].set(least)
    longest = extent.index(max(extent))
    place[longest] = (place[longest] + 1) % extent[longest]
    return drawn.at[tuple(place)].set(largest)


def strengthened(values, key, source, target, parts, factor):
    owner, partner = [(jnp.arange(values.shape[dim]) // (values.shape[dim] // parts)).reshape([-1 if axis == dim else 1 for axis in range(values.ndim)]) for dim in (source, target)]
    chosen = jax.random.permutation(key, parts)[partner]
    strong = (owner == chosen) | (owner == (partner + parts // 2) % parts)
    return jnp.where(strong, factor * values, values)


def steps_of(rng, dims, split, smallest, high):
    gain, own = 1.0, jax.random.fold_in(rng, 6)
    for position, blocks in split:
        steps = jnp.exp(jax.random.uniform(jax.random.fold_in(own, position), (blocks,), jnp.float32, smallest / len(split), high / len(split)))
        gain = gain * jnp.repeat(steps, dims[position] // blocks).reshape([-1 if axis == position else 1 for axis in range(len(dims))])
    return gain


def gaussian(own_key, shape, scale, limit, shards=(), kind=jnp.bfloat16):
    factor_of = steps_of(own_key, shape, shards, -0.22, 0.18) if shards else 1.0
    result = jax.random.normal(own_key, shape, jnp.float32) * scale * factor_of
    return jnp.minimum(jnp.maximum(result, -limit), limit).astype(kind)


def bell_draw_with(own_key, shape, spread, limit, cuts, heavy, kind=jnp.bfloat16):
    drawn = spread * jax.random.normal(own_key, shape, jnp.float32)
    if cuts:
        drawn = drawn * steps_of(own_key, shape, cuts, -0.22, 0.18)
    return jnp.clip(strengthened(drawn, jax.random.fold_in(own_key, 3), *heavy), -limit, limit).astype(kind)


def setup_inputs(seed: int = 0) -> dict:
    keys = jax.random.split(jax.random.key(seed), 5)
    partials = bell_draw_with(keys[0], (EPOCHS, P_SIZE), 1.0, 6.0, ((0, 8), (1, 4)), (0, 1, 8, 2.0))
    gaps = plant((jax.random.randint(keys[1], (EPOCHS,), 0, 8) < 7).astype(jnp.int32), jax.random.fold_in(keys[1], 1), 0, 1)
    arc_start = jax.random.randint(keys[2], (1,), EPOCHS // 4, 3 * EPOCHS // 4).astype(jnp.int32)
    taps = gaussian(keys[3], (TAPS,), TAPS ** -0.5, 0.375)
    return dict(partials=partials, gaps=gaps, arc_start=arc_start, taps=taps)


def filter_table(first, rows, halo, taps, boundary):
    width = rows + halo
    padded_taps = jnp.concatenate([taps[::-1], jnp.zeros((rows,), taps.dtype)], axis=0)
    values = jnp.tile(padded_taps, rows)[: rows * width].reshape(rows, width)
    later = jnp.arange(rows, dtype=jnp.int32)
    source = jnp.arange(width, dtype=jnp.int32)
    lag = later[:, None] + halo - source[None, :]
    arc_later = (first + later) >= boundary
    arc_source = (first - halo + source) >= boundary
    keep = (lag >= 0) & (lag <= halo) & (arc_later[:, None] == arc_source[None, :])
    return jnp.where(keep, values, jnp.zeros_like(values))


def reference(partials, gaps, arc_start, taps):
    halo = TAPS - 1
    masked = partials * gaps[:, None].astype(jnp.bfloat16)
    padded = jnp.concatenate([jnp.zeros((halo, P_SIZE), jnp.bfloat16), masked], axis=0)

    def one_block(block):
        first = (block * E_DEV).astype(jnp.int32)
        stacked = lax.dynamic_slice_in_dim(padded, first, E_DEV + halo, 0)
        table = filter_table(first, E_DEV, halo, taps, arc_start[0])
        return jnp.dot(table, stacked, preferred_element_type=jnp.float32).astype(jnp.bfloat16)

    white = lax.map(one_block, jnp.arange(EPOCHS // E_DEV, dtype=jnp.int32)).reshape(EPOCHS, P_SIZE)
    gram = jnp.dot(white.T, white, preferred_element_type=jnp.float32)
    return gram * (EPOCHS ** -0.5)
```

```python
import functools

import jax
import jax.numpy as jnp
from jax import lax
from jax.experimental import pallas as pl
from jax.experimental.pallas import tpu as pltpu
from jax.sharding import PartitionSpec as P

MESH = pl.DeviceIdType.MESH
CHUNKS = 4


def kernel(
    ne, nc, arc_ref, gaps_ref, taps_ref, part_ref, out_ref,
    left, right, table, wl, wr,
    left_recv, right_recv, up_send, dn_send, y_send, sib_send, x_send,
):
    rows, width = part_ref.shape
    rwidth = right.shape[2]
    nz, nh = ne // 2, nc // 2
    G = CHUNKS
    crows = rows // G
    e, c = lax.axis_index("epoch"), lax.axis_index("col")
    z, y = e // 2, e % 2
    h, k = c // 2, c % 2
    src = e * nc // ne
    h_src, k_src = src // 2, src % 2
    offset = pl.multiple_of((e * nc % ne) // nc * rwidth, rwidth)
    is_src = c == src
    is_relay = jnp.logical_and(k == k_src, h != h_src)
    has_up, has_dn = z < nz - 1, z > 0
    up, dn, across, sib = e + 2, e - 2, e + 1 - 2 * y, c + 1 - 2 * k

    barrier = pltpu.get_barrier_semaphore()

    def greet(ee, cc):
        pl.semaphore_signal(barrier, inc=1, device_id=(ee, cc), device_id_type=MESH)

    @pl.when(has_up)
    def _():
        greet(up, c)

    @pl.when(has_dn)
    def _():
        greet(dn, c)

    greet(across, c)
    greet(e, sib)
    for i in range(1, nh):
        greet(e, lax.rem(h + i, nh) * 2 + k)

    eye = lax.broadcasted_iota(jnp.int32, (rows, rows), 0) == lax.broadcasted_iota(jnp.int32, (rows, rows), 1)
    column = jnp.sum(jnp.where(eye, gaps_ref[...].astype(jnp.float32), 0.0), axis=1, keepdims=True)
    left[e] = part_ref[...] * column.astype(jnp.bfloat16)

    pl.semaphore_wait(barrier, 1 + nh + has_up.astype(jnp.int32) + has_dn.astype(jnp.int32))

    def piece(buf, b, g):
        return buf.at[b, pl.ds(pl.multiple_of(g * crows, crows), crows)]

    def send_left(b, g, sem, ee):
        pltpu.make_async_remote_copy(
            src_ref=piece(left, b, g), dst_ref=piece(left, b, g),
            send_sem=sem.at[b], recv_sem=left_recv.at[b, g],
            device_id=(ee, c), device_id_type=MESH,
        ).start()

    def right_source(b, g):
        return left.at[b, pl.ds(pl.multiple_of(g * crows, crows), crows), pl.ds(offset, rwidth)]

    def send_right(source, b, g, sem, cc):
        pltpu.make_async_remote_copy(
            src_ref=source, dst_ref=piece(right, b, g),
            send_sem=sem, recv_sem=right_recv.at[b, g],
            device_id=(e, cc), device_id_type=MESH,
        ).start()

    def spread(b, g):
        @pl.when(is_src)
        def _():
            pltpu.make_async_copy(right_source(b, g), piece(right, b, g), right_recv.at[b, g]).start()
            for i in range(1, nh):
                send_right(right_source(b, g), b, g, x_send.at[b, i - 1], lax.rem(h + i, nh) * 2 + k)
            send_right(right_source(b, g), b, g, sib_send.at[b], sib)

    def wait_left(b, g):
        pltpu.make_async_copy(piece(left, b, g), piece(left, b, g), left_recv.at[b, g]).wait()

    def wait_right(b, g):
        pltpu.make_async_copy(piece(right, b, g), piece(right, b, g), right_recv.at[b, g]).wait()

        @pl.when(is_relay)
        def _():
            send_right(piece(right, b, g), b, g, sib_send.at[b], sib)

    def slab(t):
        both = 2 * jnp.minimum(z, nz - 1 - z)
        alternate = jnp.where(t % 2 == 1, z - (t + 1) // 2, z + t // 2)
        rest = jnp.where(z <= nz - 1 - z, t, nz - 1 - t)
        return jnp.where(t <= both, alternate, rest)

    def own(g, carry):
        @pl.when(has_up)
        def _():
            send_left(e, g, up_send, up)

        @pl.when(has_dn)
        def _():
            send_left(e, g, dn_send, dn)

        send_left(e, g, y_send, across)
        spread(e, g)
        return carry

    lax.fori_loop(0, G, own, 0)

    table[...] = pltpu.roll(
        jnp.broadcast_to(taps_ref[...], (rows, 2 * rows)), 0, 1, stride=1, stride_axis=0
    )
    out_ref[...] = jnp.zeros_like(out_ref)

    def whiten_and_add(b):
        first = b * rows
        before = jnp.maximum(b - 1, 0)
        later = first + lax.broadcasted_iota(jnp.int32, (rows, 2 * rows), 0)
        source = first - rows + lax.broadcasted_iota(jnp.int32, (rows, 2 * rows), 1)
        boundary = arc_ref[0]
        same = (later >= boundary) == (source >= boundary)
        keep = jnp.logical_and(same, source >= 0)
        taps = jnp.where(keep, table[...], 0.0).astype(jnp.bfloat16)
        edge, inner = taps[:, :rows], taps[:, rows:]

        def whiten(buf, into, step):
            @pl.loop(0, into.shape[1] // step)
            def _(i):
                cols = pl.ds(pl.multiple_of(i * step, step), step)
                white = jnp.dot(inner, buf[b, :, cols], preferred_element_type=jnp.float32)
                white += jnp.dot(edge, buf[before, :, cols], preferred_element_type=jnp.float32)
                into[:, cols] = white.astype(jnp.bfloat16)

        whiten(left, wl, min(512, width))
        whiten(right, wr, min(512, rwidth))

        @pl.loop(0, width // 256)
        def _(i):
            cols = pl.ds(pl.multiple_of(i * 256, 256), 256)
            out_ref[cols, :] += lax.dot_general(
                wl[:, cols], wr[...], (((0,), (0,)), ((), ())), preferred_element_type=jnp.float32
            )

    def step(it, carry):
        t, g = it // G, it % G
        moving = t < nz

        @pl.when(jnp.logical_and(moving, z - t - 1 >= 0))
        def _():
            b = e - 2 * (t + 1)
            wait_left(b, g)

            @pl.when(has_up)
            def _():
                send_left(b, g, up_send, up)

            spread(b, g)

        @pl.when(jnp.logical_and(moving, z + t + 1 < nz))
        def _():
            b = e + 2 * (t + 1)
            wait_left(b, g)

            @pl.when(has_dn)
            def _():
                send_left(b, g, dn_send, dn)

            spread(b, g)

        @pl.when(t + 1 < nz)
        def _():
            send_left(2 * slab(t + 1) + y, g, y_send, across)

        @pl.when(moving)
        def _():
            b = 2 * slab(t) + 1 - y
            wait_left(b, g)
            spread(b, g)

        @pl.when(t == 0)
        def _():
            wait_right(e, g)

        last = jnp.maximum(it - 1, 0)
        pt, pg = last // G, last % G
        passed = jnp.logical_and(it >= 1, pt < nz)

        @pl.when(jnp.logical_and(passed, z - pt - 1 >= 0))
        def _():
            wait_right(e - 2 * (pt + 1), pg)

        @pl.when(jnp.logical_and(passed, z + pt + 1 < nz))
        def _():
            wait_right(e + 2 * (pt + 1), pg)

        @pl.when(passed)
        def _():
            wait_right(2 * slab(pt) + 1 - y, pg)

        s = slab(jnp.maximum(t - 1, 0))
        s_now = slab(jnp.minimum(t, nz - 1))
        below = s < z
        post_a = jnp.where(s > z, 2 * s + 1 - y, 2 * s + 1)
        post_b = jnp.where(
            s > z,
            2 * s + 1,
            jnp.where(jnp.logical_and(below, y == 0), 2 * s + 2, 0),
        )
        valid_b = jnp.where(
            s > z,
            y == 1,
            jnp.where(below, jnp.logical_or(y == 0, s == 0), s == 0),
        )
        pre = jnp.where(s_now > z, 2 * s_now, jnp.where(y == 0, 0, 2 * s_now + 2))
        valid_pre = jnp.where(
            s_now > z, y == 0, jnp.logical_and(s_now < z, jnp.logical_or(y == 1, s_now == 0))
        )
        task = jnp.where(g == 0, post_a, jnp.where(g == 1, post_b, pre))
        valid = jnp.logical_or(
            jnp.logical_and(t >= 1, jnp.logical_or(g == 0, jnp.logical_and(g == 1, valid_b))),
            jnp.logical_and(jnp.logical_and(moving, t >= 1), jnp.logical_and(g == 2, valid_pre)),
        )

        @pl.when(valid)
        def _():
            whiten_and_add(task)

        return carry

    lax.fori_loop(0, nz * G + 2, step, 0)

    def drain(b, carry):
        def sent(buf, sem):
            pltpu.make_async_copy(buf.at[b], buf.at[b], sem).wait()

        mine = b % 2 == y

        @pl.when(jnp.logical_and(mine, jnp.logical_and(has_up, b <= e)))
        def _():
            sent(left, up_send.at[b])

        @pl.when(jnp.logical_and(mine, jnp.logical_and(has_dn, b >= e)))
        def _():
            sent(left, dn_send.at[b])

        @pl.when(mine)
        def _():
            sent(left, y_send.at[b])

        @pl.when(is_src)
        def _():
            for i in range(1, nh):
                sent(right, x_send.at[b, i - 1])

        @pl.when(jnp.logical_or(is_src, is_relay))
        def _():
            sent(right, sib_send.at[b])

        return carry

    lax.fori_loop(0, ne, drain, 0)


def on_device(ne, nc, partials, gaps, arc_start, taps):
    rows, width = partials.shape
    rwidth = width * nc // ne
    halo = taps.shape[0] - 1
    lags = jnp.pad(taps[::-1].astype(jnp.float32), (rows - halo, rows - 1))[None, :]
    vmem = pl.BlockSpec(memory_space=pltpu.VMEM)
    gram = pl.pallas_call(
        functools.partial(kernel, ne, nc),
        out_shape=jax.ShapeDtypeStruct((width, rwidth), jnp.float32),
        in_specs=[pl.BlockSpec(memory_space=pltpu.SMEM), vmem, vmem, vmem],
        out_specs=vmem,
        scratch_shapes=[
            pltpu.VMEM((ne, rows, width), jnp.bfloat16),
            pltpu.VMEM((ne, rows, rwidth), jnp.bfloat16),
            pltpu.VMEM((rows, 2 * rows), jnp.float32),
            pltpu.VMEM((rows, width), jnp.bfloat16),
            pltpu.VMEM((rows, rwidth), jnp.bfloat16),
            pltpu.SemaphoreType.DMA((ne, CHUNKS)),
            pltpu.SemaphoreType.DMA((ne, CHUNKS)),
            pltpu.SemaphoreType.DMA((ne,)),
            pltpu.SemaphoreType.DMA((ne,)),
            pltpu.SemaphoreType.DMA((ne,)),
            pltpu.SemaphoreType.DMA((ne,)),
            pltpu.SemaphoreType.DMA((ne, nc // 2)),
        ],
        compiler_params=pltpu.CompilerParams(
            collective_id=0, has_side_effects=True, vmem_limit_bytes=48 * 1024 * 1024
        ),
        cost_estimate=pl.CostEstimate(
            flops=2 * ne * rows * width * rwidth, bytes_accessed=4 * width * rwidth, transcendentals=0
        ),
    )(arc_start, gaps[None, :], lags, partials)
    return gram * (rows * ne) ** (-0.5)


def solution(mesh):
    in_specs = (P("epoch", "col"), P("epoch"), P(), P())
    out_specs = P("col", "epoch")
    ne, nc = mesh.shape["epoch"], mesh.shape["col"]
    return jax.shard_map(
        functools.partial(on_device, ne, nc),
        mesh=mesh, in_specs=in_specs, out_specs=out_specs, check_vma=False,
    )
```

```python
import functools

import jax
import jax.numpy as jnp
from jax import lax
from jax.experimental import pallas as pl
from jax.experimental.pallas import tpu as pltpu
from jax.sharding import PartitionSpec as P

MESH = pl.DeviceIdType.MESH
CHUNKS = 4


def kernel(
    ne, nc, arc_ref, gaps_ref, taps_ref, part_ref, out_ref,
    left, right, table, wl, wr, gaps_here, taps_here,
    left_recv, right_recv, up_send, dn_send, y_send, sib_send, x_send, in_sem,
):
    rows, width = part_ref.shape
    rwidth = right.shape[2]
    nz, nh = ne // 2, nc // 2
    G = CHUNKS
    crows = rows // G
    e, c = lax.axis_index("epoch"), lax.axis_index("col")
    z, y = e // 2, e % 2
    h, k = c // 2, c % 2
    src = e * nc // ne
    h_src, k_src = src // 2, src % 2
    offset = pl.multiple_of((e * nc % ne) // nc * rwidth, rwidth)
    is_src = c == src
    is_relay = jnp.logical_and(k == k_src, h != h_src)
    has_up, has_dn = z < nz - 1, z > 0
    up, dn, across, sib = e + 2, e - 2, e + 1 - 2 * y, c + 1 - 2 * k

    low, high = z == 0, z == nz - 1
    near_low, near_high = z == 1, z == nz - 2
    end, near = jnp.logical_or(low, high), jnp.logical_or(near_low, near_high)
    slabs = jnp.where(near, nz - 1, nz)
    far = jnp.where(z <= 1, nz - 1, 0)
    beside = jnp.where(z <= 1, 0, nz - 1)

    load_rows = pltpu.make_async_copy(part_ref, left.at[e], in_sem.at[0])
    load_gaps = pltpu.make_async_copy(gaps_ref, gaps_here, in_sem.at[1])
    load_taps = pltpu.make_async_copy(taps_ref, taps_here, in_sem.at[2])
    load_rows.start()
    load_gaps.start()
    load_taps.start()
    barrier = pltpu.get_barrier_semaphore()

    def greet(ee, cc):
        pl.semaphore_signal(barrier, inc=1, device_id=(ee, cc), device_id_type=MESH)

    @pl.when(has_up)
    def _():
        greet(up, c)

    @pl.when(has_dn)
    def _():
        greet(dn, c)

    greet(across, c)
    greet(e, sib)
    for i in range(1, nh):
        greet(e, lax.rem(h + i, nh) * 2 + k)

    load_rows.wait()
    load_gaps.wait()
    load_taps.wait()
    eye = lax.broadcasted_iota(jnp.int32, (rows, rows), 0) == lax.broadcasted_iota(jnp.int32, (rows, rows), 1)
    column = jnp.sum(jnp.where(eye, gaps_here[...].astype(jnp.float32), 0.0), axis=1, keepdims=True)
    left[e] = left[e] * column.astype(jnp.bfloat16)

    pl.semaphore_wait(barrier, 1 + nh + has_up.astype(jnp.int32) + has_dn.astype(jnp.int32))

    def piece(buf, b, g):
        return buf.at[b, pl.ds(pl.multiple_of(g * crows, crows), crows)]

    def send_left(b, g, sem, ee):
        pltpu.make_async_remote_copy(
            src_ref=piece(left, b, g), dst_ref=piece(left, b, g),
            send_sem=sem.at[b], recv_sem=left_recv.at[b, g],
            device_id=(ee, c), device_id_type=MESH,
        ).start()

    def right_source(b, g):
        return left.at[b, pl.ds(pl.multiple_of(g * crows, crows), crows), pl.ds(offset, rwidth)]

    def send_right(source, b, g, sem, cc):
        pltpu.make_async_remote_copy(
            src_ref=source, dst_ref=piece(right, b, g),
            send_sem=sem, recv_sem=right_recv.at[b, g],
            device_id=(e, cc), device_id_type=MESH,
        ).start()

    def spread(b, g):
        @pl.when(is_src)
        def _():
            pltpu.make_async_copy(right_source(b, g), piece(right, b, g), right_recv.at[b, g]).start()
            for i in range(1, nh):
                send_right(right_source(b, g), b, g, x_send.at[b, i - 1], lax.rem(h + i, nh) * 2 + k)
            send_right(right_source(b, g), b, g, sib_send.at[b], sib)

    def wait_left(b, g):
        pltpu.make_async_copy(piece(left, b, g), piece(left, b, g), left_recv.at[b, g]).wait()

    def wait_right(b, g):
        pltpu.make_async_copy(piece(right, b, g), piece(right, b, g), right_recv.at[b, g]).wait()

        @pl.when(is_relay)
        def _():
            send_right(piece(right, b, g), b, g, sib_send.at[b], sib)

    def slab(t):
        both = 2 * jnp.minimum(z, nz - 1 - z)
        alternate = jnp.where(t % 2 == 1, z - (t + 1) // 2, z + t // 2)
        rest = jnp.where(z <= nz - 1 - z, t, nz - 1 - t)
        middle = jnp.where(t <= both, alternate, rest)
        return jnp.where(z <= 1, z + t, jnp.where(z >= nz - 2, z - t, middle))

    def own(g, carry):
        @pl.when(has_up)
        def _():
            send_left(e, g, up_send, up)

        @pl.when(has_dn)
        def _():
            send_left(e, g, dn_send, dn)

        send_left(e, g, y_send, across)
        spread(e, g)
        return carry

    lax.fori_loop(0, G, own, 0)

    lags = pltpu.roll(
        jnp.broadcast_to(taps_here[...], (2 * rows, 2 * rows)), 0, 1, stride=1, stride_axis=0
    )
    table[...] = lags[:, :rows].T
    out_ref[...] = jnp.zeros_like(out_ref)

    def whiten_and_add(b):
        first = b * rows
        before = jnp.maximum(b - 1, 0)
        later = first + lax.broadcasted_iota(jnp.int32, (rows, 2 * rows), 0)
        source = first - rows + lax.broadcasted_iota(jnp.int32, (rows, 2 * rows), 1)
        boundary = arc_ref[0]
        same = (later >= boundary) == (source >= boundary)
        keep = jnp.logical_and(same, source >= 0)
        taps = jnp.where(keep, table[...], 0.0).astype(jnp.bfloat16)
        edge, inner = taps[:, :rows], taps[:, rows:]

        def whiten(buf, into, step):
            @pl.loop(0, into.shape[1] // step)
            def _(i):
                cols = pl.ds(pl.multiple_of(i * step, step), step)
                white = jnp.dot(inner, buf[b, :, cols], preferred_element_type=jnp.float32)
                white += jnp.dot(edge, buf[before, :, cols], preferred_element_type=jnp.float32)
                into[:, cols] = white.astype(jnp.bfloat16)

        whiten(left, wl, min(512, width))
        whiten(right, wr, min(512, rwidth))

        @pl.loop(0, width // 256)
        def _(i):
            cols = pl.ds(pl.multiple_of(i * 256, 256), 256)
            out_ref[cols, :] += lax.dot_general(
                wl[:, cols], wr[...], (((0,), (0,)), ((), ())), preferred_element_type=jnp.float32
            )

    def step(it, carry):
        t, g = it // G, it % G
        moving = t < nz

        @pl.when(jnp.logical_and(moving, z - t - 1 >= 0))
        def _():
            b = e - 2 * (t + 1)
            wait_left(b, g)

            @pl.when(has_up)
            def _():
                send_left(b, g, up_send, up)

            spread(b, g)

        @pl.when(jnp.logical_and(moving, z + t + 1 < nz))
        def _():
            b = e + 2 * (t + 1)
            wait_left(b, g)

            @pl.when(has_dn)
            def _():
                send_left(b, g, dn_send, dn)

            spread(b, g)

        by_y = jnp.logical_or(t + 1 < nz - 1, jnp.logical_or(jnp.logical_not(end), g < G // 2))

        @pl.when(jnp.logical_and(t + 1 < slabs, by_y))
        def _():
            send_left(2 * slab(t + 1) + y, g, y_send, across)

        @pl.when(t < slabs)
        def _():
            b = 2 * slab(t) + 1 - y
            wait_left(b, g)
            to_near = jnp.logical_and(end, t == 0)
            to_end = jnp.logical_and(near, jnp.logical_and(t == nz - 2, g >= G // 2))

            @pl.when(jnp.logical_or(jnp.logical_and(low, to_near), jnp.logical_and(near_high, to_end)))
            def _():
                send_left(b, g, up_send, up)

            @pl.when(jnp.logical_or(jnp.logical_and(high, to_near), jnp.logical_and(near_low, to_end)))
            def _():
                send_left(b, g, dn_send, dn)

            spread(b, g)

        @pl.when(jnp.logical_and(near, t == 1))
        def _():
            b = 2 * beside + 1 - y
            wait_left(b, g)
            spread(b, g)

        @pl.when(t == 0)
        def _():
            wait_right(e, g)

        last = jnp.maximum(it - 1, 0)
        pt, pg = last // G, last % G
        passed = jnp.logical_and(it >= 1, pt < nz)

        @pl.when(jnp.logical_and(passed, z - pt - 1 >= 0))
        def _():
            wait_right(e - 2 * (pt + 1), pg)

        @pl.when(jnp.logical_and(passed, z + pt + 1 < nz))
        def _():
            wait_right(e + 2 * (pt + 1), pg)

        @pl.when(jnp.logical_and(it >= 1, pt < slabs))
        def _():
            wait_right(2 * slab(pt) + 1 - y, pg)

        @pl.when(jnp.logical_and(it >= 1, jnp.logical_and(near, pt == 1)))
        def _():
            wait_right(2 * beside + 1 - y, pg)

        s = slab(jnp.clip(t - 1, 0, slabs - 1))
        s_now = slab(jnp.minimum(t, slabs - 1))
        below = s < z
        post_a = jnp.where(s > z, 2 * s + 1 - y, 2 * s + 1)
        post_b = jnp.where(
            s > z,
            2 * s + 1,
            jnp.where(jnp.logical_and(below, y == 0), 2 * s + 2, 0),
        )
        valid_b = jnp.where(
            s > z,
            y == 1,
            jnp.where(below, jnp.logical_or(y == 0, s == 0), s == 0),
        )
        pre = jnp.where(s_now > z, 2 * s_now, jnp.where(y == 0, 0, 2 * s_now + 2))
        valid_pre = jnp.where(
            s_now > z, y == 0, jnp.logical_and(s_now < z, jnp.logical_or(y == 1, s_now == 0))
        )
        free = jnp.where(near_low == (y == 0), 1, 2)
        early = jnp.logical_and(t == 1, g == 3)
        middling = jnp.logical_and(t == 2, g == free)
        late = jnp.logical_and(t == 2, g == 3)
        first_low = jnp.where(y == 0, 0, 2)
        middling_low, late_low = jnp.where(y == 0, 2, 0), 1
        middling_high, late_high = ne - 2, ne - 1
        extra = jnp.where(
            near_low,
            jnp.where(early, first_low, jnp.where(late, late_low, middling_low)),
            jnp.where(jnp.logical_or(early, middling), middling_high, late_high),
        )
        valid_extra = jnp.where(
            near_low,
            jnp.logical_or(early, jnp.logical_or(middling, late)),
            jnp.logical_and(
                near_high,
                jnp.logical_or(late, jnp.where(y == 0, early, middling)),
            ),
        )
        valid_post = jnp.logical_and(
            jnp.logical_and(t >= 1, t <= slabs),
            jnp.logical_or(g == 0, jnp.logical_and(g == 1, valid_b)),
        )
        valid_pre = jnp.logical_and(jnp.logical_and(t >= 1, t < slabs), jnp.logical_and(g == 2, valid_pre))
        task = jnp.where(g == 0, post_a, jnp.where(g == 1, post_b, pre))
        task = jnp.where(valid_extra, extra, task)
        valid = jnp.logical_or(valid_extra, jnp.logical_or(valid_post, valid_pre))

        @pl.when(valid)
        def _():
            whiten_and_add(task)

        return carry

    lax.fori_loop(0, nz * G + 2, step, 0)

    def drain(b, carry):
        def sent(buf, sem, part=rows):
            span = buf.at[b, pl.ds(0, part)]
            pltpu.make_async_copy(span, span, sem).wait()

        mine = b % 2 == y
        whole_b = jnp.logical_and(end, b == e + 1 - 2 * y)
        half_b = jnp.logical_and(near, b == 2 * far + 1 - y)

        @pl.when(jnp.logical_or(jnp.logical_and(mine, jnp.logical_and(has_up, b <= e)), jnp.logical_and(low, whole_b)))
        def _():
            sent(left, up_send.at[b])

        @pl.when(jnp.logical_or(jnp.logical_and(mine, jnp.logical_and(has_dn, b >= e)), jnp.logical_and(high, whole_b)))
        def _():
            sent(left, dn_send.at[b])

        @pl.when(jnp.logical_and(near_high, half_b))
        def _():
            sent(left, up_send.at[b], rows // 2)

        @pl.when(jnp.logical_and(near_low, half_b))
        def _():
            sent(left, dn_send.at[b], rows // 2)

        halved = jnp.logical_and(end, b == 2 * far + y)
        skipped = jnp.logical_and(near, b == 2 * beside + y)

        @pl.when(jnp.logical_and(mine, jnp.logical_not(jnp.logical_or(halved, skipped))))
        def _():
            sent(left, y_send.at[b])

        @pl.when(halved)
        def _():
            sent(left, y_send.at[b], rows // 2)

        @pl.when(is_src)
        def _():
            for i in range(1, nh):
                sent(right, x_send.at[b, i - 1])

        @pl.when(jnp.logical_or(is_src, is_relay))
        def _():
            sent(right, sib_send.at[b])

        return carry

    lax.fori_loop(0, ne, drain, 0)


def on_device(ne, nc, partials, gaps, arc_start, taps):
    rows, width = partials.shape
    rwidth = width * nc // ne
    lags = jnp.pad(taps.astype(jnp.float32), (rows, rows - taps.shape[0]))[None, :]
    hbm = pl.BlockSpec(memory_space=pl.ANY)
    gram = pl.pallas_call(
        functools.partial(kernel, ne, nc),
        out_shape=pltpu.VMEM((width, rwidth), jnp.float32),
        in_specs=[pl.BlockSpec(memory_space=pltpu.SMEM), hbm, hbm, hbm],
        out_specs=pl.BlockSpec(memory_space=pltpu.VMEM),
        scratch_shapes=[
            pltpu.VMEM((ne, rows, width), jnp.bfloat16),
            pltpu.VMEM((ne, rows, rwidth), jnp.bfloat16),
            pltpu.VMEM((rows, 2 * rows), jnp.float32),
            pltpu.VMEM((rows, width), jnp.bfloat16),
            pltpu.VMEM((rows, rwidth), jnp.bfloat16),
            pltpu.VMEM((1, rows), jnp.int32),
            pltpu.VMEM((1, 2 * rows), jnp.float32),
            pltpu.SemaphoreType.DMA((ne, CHUNKS)),
            pltpu.SemaphoreType.DMA((ne, CHUNKS)),
            pltpu.SemaphoreType.DMA((ne,)),
            pltpu.SemaphoreType.DMA((ne,)),
            pltpu.SemaphoreType.DMA((ne,)),
            pltpu.SemaphoreType.DMA((ne,)),
            pltpu.SemaphoreType.DMA((ne, nc // 2)),
            pltpu.SemaphoreType.DMA((3,)),
        ],
        compiler_params=pltpu.CompilerParams(
            collective_id=0, has_side_effects=True, vmem_limit_bytes=48 * 1024 * 1024
        ),
        cost_estimate=pl.CostEstimate(
            flops=2 * ne * rows * width * rwidth, bytes_accessed=4 * width * rwidth, transcendentals=0
        ),
    )(arc_start, gaps[None, :], lags, partials)
    return gram * (rows * ne) ** (-0.5)


def solution(mesh):
    in_specs = (P("epoch", "col"), P("epoch"), P(), P())
    out_specs = P("col", "epoch")
    ne, nc = mesh.shape["epoch"], mesh.shape["col"]
    return jax.shard_map(
        functools.partial(on_device, ne, nc),
        mesh=mesh, in_specs=in_specs, out_specs=out_specs, check_vma=False,
    )
```

```python
import functools

import jax
import jax.numpy as jnp
from jax import lax
from jax.experimental import pallas as pl
from jax.experimental.pallas import tpu as pltpu
from jax.sharding import PartitionSpec as P

MESH = pl.DeviceIdType.MESH
CHUNKS = 4


def kernel(
    ne, nc, arc_ref, gaps_ref, taps_ref, part_ref, out_ref, wl_last, wr_last,
    left, right, table, wl, wr, gaps_here, taps_here,
    left_recv, right_recv, up_send, dn_send, y_send, sib_send, x_send, x_last, in_sem,
):
    rows, width = part_ref.shape
    rwidth = right.shape[2]
    nz, nh = ne // 2, nc // 2
    G = CHUNKS
    crows = rows // G
    e, c = lax.axis_index("epoch"), lax.axis_index("col")
    z, y = e // 2, e % 2
    h, k = c // 2, c % 2
    src = e * nc // ne
    h_src, k_src = src // 2, src % 2
    offset = pl.multiple_of((e * nc % ne) // nc * rwidth, rwidth)
    is_src = c == src
    is_relay = jnp.logical_and(k == k_src, h != h_src)
    has_up, has_dn = z < nz - 1, z > 0
    up, dn, across, sib = e + 2, e - 2, e + 1 - 2 * y, c + 1 - 2 * k

    low, high = z == 0, z == nz - 1
    near_low, near_high = z == 1, z == nz - 2
    end, near = jnp.logical_or(low, high), jnp.logical_or(near_low, near_high)
    slabs = jnp.where(near, nz - 1, nz)
    far = jnp.where(z <= 1, nz - 1, 0)
    beside = jnp.where(z <= 1, 0, nz - 1)

    load_rows = pltpu.make_async_copy(part_ref, left.at[e], in_sem.at[0])
    load_gaps = pltpu.make_async_copy(gaps_ref, gaps_here, in_sem.at[1])
    load_taps = pltpu.make_async_copy(taps_ref, taps_here, in_sem.at[2])
    load_rows.start()
    load_gaps.start()
    load_taps.start()
    barrier = pltpu.get_barrier_semaphore()

    def greet(ee, cc):
        pl.semaphore_signal(barrier, inc=1, device_id=(ee, cc), device_id_type=MESH)

    @pl.when(has_up)
    def _():
        greet(up, c)

    @pl.when(has_dn)
    def _():
        greet(dn, c)

    greet(across, c)
    for i in range(1, nc):
        greet(e, lax.rem(c + i, nc))

    load_rows.wait()
    load_gaps.wait()
    load_taps.wait()
    eye = lax.broadcasted_iota(jnp.int32, (rows, rows), 0) == lax.broadcasted_iota(jnp.int32, (rows, rows), 1)
    column = jnp.sum(jnp.where(eye, gaps_here[...].astype(jnp.float32), 0.0), axis=1, keepdims=True)
    left[e] = left[e] * column.astype(jnp.bfloat16)

    pl.semaphore_wait(barrier, nc + has_up.astype(jnp.int32) + has_dn.astype(jnp.int32))

    def slab(t):
        both = 2 * jnp.minimum(z, nz - 1 - z)
        alternate = jnp.where(t % 2 == 1, z - (t + 1) // 2, z + t // 2)
        rest = jnp.where(z <= nz - 1 - z, t, nz - 1 - t)
        middle = jnp.where(t <= both, alternate, rest)
        return jnp.where(z <= 1, z + t, jnp.where(z >= nz - 2, z - t, middle))

    b_last = 2 * slab(slabs - 1) + 1 - y

    def piece(buf, b, g):
        return buf.at[b, pl.ds(pl.multiple_of(g * crows, crows), crows)]

    def send_left(b, g, sem, ee):
        pltpu.make_async_remote_copy(
            src_ref=piece(left, b, g), dst_ref=piece(left, b, g),
            send_sem=sem.at[b], recv_sem=left_recv.at[b, g],
            device_id=(ee, c), device_id_type=MESH,
        ).start()

    def right_source(b, g):
        return left.at[b, pl.ds(pl.multiple_of(g * crows, crows), crows), pl.ds(offset, rwidth)]

    def send_right(source, b, g, sem, cc):
        pltpu.make_async_remote_copy(
            src_ref=source, dst_ref=piece(right, b, g),
            send_sem=sem, recv_sem=right_recv.at[b, g],
            device_id=(e, cc), device_id_type=MESH,
        ).start()

    def spread(b, g):
        @pl.when(is_src)
        def _():
            pltpu.make_async_copy(right_source(b, g), piece(right, b, g), right_recv.at[b, g]).start()
            for i in range(1, nh):
                send_right(right_source(b, g), b, g, x_send.at[b, i - 1], lax.rem(h + i, nh) * 2 + k)
            send_right(right_source(b, g), b, g, sib_send.at[b], sib)

            @pl.when(b == b_last)
            def _():
                for i in range(1, nh):
                    send_right(right_source(b, g), b, g, x_last.at[i - 1], lax.rem(h + i, nh) * 2 + 1 - k)

    def wait_left(b, g):
        pltpu.make_async_copy(piece(left, b, g), piece(left, b, g), left_recv.at[b, g]).wait()

    def wait_right(b, g):
        pltpu.make_async_copy(piece(right, b, g), piece(right, b, g), right_recv.at[b, g]).wait()

        @pl.when(jnp.logical_and(is_relay, b != b_last))
        def _():
            send_right(piece(right, b, g), b, g, sib_send.at[b], sib)

    def own(g, carry):
        @pl.when(has_up)
        def _():
            send_left(e, g, up_send, up)

        @pl.when(has_dn)
        def _():
            send_left(e, g, dn_send, dn)

        send_left(e, g, y_send, across)
        spread(e, g)
        return carry

    lax.fori_loop(0, G, own, 0)

    lags = pltpu.roll(
        jnp.broadcast_to(taps_here[...], (2 * rows, 2 * rows)), 0, 1, stride=1, stride_axis=0
    )
    table[...] = lags[:, :rows].T
    out_ref[...] = jnp.zeros_like(out_ref)
    wl_last[1] = jnp.zeros((rows, width), jnp.bfloat16)
    wr_last[1] = jnp.zeros((rows, rwidth), jnp.bfloat16)

    def whiten_into(b, into_left, into_right):
        first = b * rows
        before = jnp.maximum(b - 1, 0)
        later = first + lax.broadcasted_iota(jnp.int32, (rows, 2 * rows), 0)
        source = first - rows + lax.broadcasted_iota(jnp.int32, (rows, 2 * rows), 1)
        boundary = arc_ref[0]
        same = (later >= boundary) == (source >= boundary)
        keep = jnp.logical_and(same, source >= 0)
        taps = jnp.where(keep, table[...], 0.0).astype(jnp.bfloat16)
        edge, inner = taps[:, :rows], taps[:, rows:]

        def whiten(buf, into, step):
            @pl.loop(0, into.shape[1] // step)
            def _(i):
                cols = pl.ds(pl.multiple_of(i * step, step), step)
                white = jnp.dot(inner, buf[b, :, cols], preferred_element_type=jnp.float32)
                white += jnp.dot(edge, buf[before, :, cols], preferred_element_type=jnp.float32)
                into[:, cols] = white.astype(jnp.bfloat16)

        whiten(left, into_left, min(512, width))
        whiten(right, into_right, min(512, rwidth))

    def whiten_and_add(b):
        whiten_into(b, wl, wr)

        @pl.loop(0, width // 256)
        def _(i):
            cols = pl.ds(pl.multiple_of(i * 256, 256), 256)
            out_ref[cols, :] += lax.dot_general(
                wl[:, cols], wr[...], (((0,), (0,)), ((), ())), preferred_element_type=jnp.float32
            )

    def step(it, carry):
        t, g = it // G, it % G
        moving = t < nz

        @pl.when(jnp.logical_and(moving, z - t - 1 >= 0))
        def _():
            b = e - 2 * (t + 1)
            wait_left(b, g)

            @pl.when(has_up)
            def _():
                send_left(b, g, up_send, up)

            spread(b, g)

        @pl.when(jnp.logical_and(moving, z + t + 1 < nz))
        def _():
            b = e + 2 * (t + 1)
            wait_left(b, g)

            @pl.when(has_dn)
            def _():
                send_left(b, g, dn_send, dn)

            spread(b, g)

        by_y = jnp.logical_or(t + 1 < nz - 1, jnp.logical_or(jnp.logical_not(end), g < G // 2))

        @pl.when(jnp.logical_and(t + 1 < slabs, by_y))
        def _():
            send_left(2 * slab(t + 1) + y, g, y_send, across)

        @pl.when(t < slabs)
        def _():
            b = 2 * slab(t) + 1 - y
            wait_left(b, g)
            to_near = jnp.logical_and(end, t == 0)
            to_end = jnp.logical_and(near, jnp.logical_and(t == nz - 2, g >= G // 2))

            @pl.when(jnp.logical_or(jnp.logical_and(low, to_near), jnp.logical_and(near_high, to_end)))
            def _():
                send_left(b, g, up_send, up)

            @pl.when(jnp.logical_or(jnp.logical_and(high, to_near), jnp.logical_and(near_low, to_end)))
            def _():
                send_left(b, g, dn_send, dn)

            spread(b, g)

        @pl.when(jnp.logical_and(near, t == 1))
        def _():
            b = 2 * beside + 1 - y
            wait_left(b, g)
            spread(b, g)

        @pl.when(t == 0)
        def _():
            wait_right(e, g)

        last = jnp.maximum(it - 1, 0)
        pt, pg = last // G, last % G
        passed = jnp.logical_and(it >= 1, pt < nz)

        @pl.when(jnp.logical_and(passed, z - pt - 1 >= 0))
        def _():
            wait_right(e - 2 * (pt + 1), pg)

        @pl.when(jnp.logical_and(passed, z + pt + 1 < nz))
        def _():
            wait_right(e + 2 * (pt + 1), pg)

        @pl.when(jnp.logical_and(it >= 1, pt < slabs))
        def _():
            wait_right(2 * slab(pt) + 1 - y, pg)

        @pl.when(jnp.logical_and(it >= 1, jnp.logical_and(near, pt == 1)))
        def _():
            wait_right(2 * beside + 1 - y, pg)

        s = slab(jnp.clip(t - 1, 0, slabs - 1))
        s_now = slab(jnp.minimum(t, slabs - 1))
        below = s < z
        post_a = jnp.where(s > z, 2 * s + 1 - y, 2 * s + 1)
        post_b = jnp.where(
            s > z,
            2 * s + 1,
            jnp.where(jnp.logical_and(below, y == 0), 2 * s + 2, 0),
        )
        valid_b = jnp.where(
            s > z,
            y == 1,
            jnp.where(below, jnp.logical_or(y == 0, s == 0), s == 0),
        )
        pre = jnp.where(s_now > z, 2 * s_now, jnp.where(y == 0, 0, 2 * s_now + 2))
        valid_pre = jnp.where(
            s_now > z, y == 0, jnp.logical_and(s_now < z, jnp.logical_or(y == 1, s_now == 0))
        )
        free = jnp.where(near_low == (y == 0), 1, 2)
        early = jnp.logical_and(t == 1, g == 3)
        middling = jnp.logical_and(t == 2, g == free)
        late = jnp.logical_and(t == 2, g == 3)
        first_low = jnp.where(y == 0, 0, 2)
        middling_low, late_low = jnp.where(y == 0, 2, 0), 1
        middling_high, late_high = ne - 2, ne - 1
        extra = jnp.where(
            near_low,
            jnp.where(early, first_low, jnp.where(late, late_low, middling_low)),
            jnp.where(jnp.logical_or(early, middling), middling_high, late_high),
        )
        valid_extra = jnp.where(
            near_low,
            jnp.logical_or(early, jnp.logical_or(middling, late)),
            jnp.logical_and(
                near_high,
                jnp.logical_or(late, jnp.where(y == 0, early, middling)),
            ),
        )
        valid_post = jnp.logical_and(
            jnp.logical_and(t >= 1, t <= slabs),
            jnp.logical_or(g == 0, jnp.logical_and(g == 1, valid_b)),
        )
        valid_pre = jnp.logical_and(jnp.logical_and(t >= 1, t < slabs), jnp.logical_and(g == 2, valid_pre))
        task = jnp.where(g == 0, post_a, jnp.where(g == 1, post_b, pre))
        task = jnp.where(valid_extra, extra, task)
        valid = jnp.logical_or(valid_extra, jnp.logical_or(valid_post, valid_pre))

        tail = t == slabs

        @pl.when(jnp.logical_and(valid, jnp.logical_not(tail)))
        def _():
            whiten_and_add(task)

        @pl.when(jnp.logical_and(valid, tail))
        def _():
            whiten_into(task, wl_last.at[g], wr_last.at[g])

        return carry

    lax.fori_loop(0, nz * G + 2, step, 0)

    def drain(b, carry):
        def sent(buf, sem, part=rows):
            span = buf.at[b, pl.ds(0, part)]
            pltpu.make_async_copy(span, span, sem).wait()

        mine = b % 2 == y
        whole_b = jnp.logical_and(end, b == e + 1 - 2 * y)
        half_b = jnp.logical_and(near, b == 2 * far + 1 - y)

        @pl.when(jnp.logical_or(jnp.logical_and(mine, jnp.logical_and(has_up, b <= e)), jnp.logical_and(low, whole_b)))
        def _():
            sent(left, up_send.at[b])

        @pl.when(jnp.logical_or(jnp.logical_and(mine, jnp.logical_and(has_dn, b >= e)), jnp.logical_and(high, whole_b)))
        def _():
            sent(left, dn_send.at[b])

        @pl.when(jnp.logical_and(near_high, half_b))
        def _():
            sent(left, up_send.at[b], rows // 2)

        @pl.when(jnp.logical_and(near_low, half_b))
        def _():
            sent(left, dn_send.at[b], rows // 2)

        halved = jnp.logical_and(end, b == 2 * far + y)
        skipped = jnp.logical_and(near, b == 2 * beside + y)

        @pl.when(jnp.logical_and(mine, jnp.logical_not(jnp.logical_or(halved, skipped))))
        def _():
            sent(left, y_send.at[b])

        @pl.when(halved)
        def _():
            sent(left, y_send.at[b], rows // 2)

        @pl.when(is_src)
        def _():
            for i in range(1, nh):
                sent(right, x_send.at[b, i - 1])

        @pl.when(jnp.logical_or(is_src, jnp.logical_and(is_relay, b != b_last)))
        def _():
            sent(right, sib_send.at[b])

        @pl.when(jnp.logical_and(is_src, b == b_last))
        def _():
            for i in range(1, nh):
                sent(right, x_last.at[i - 1])

        return carry

    lax.fori_loop(0, ne, drain, 0)


def finish(tile, scale, gram_ref, wl_ref, wr_ref, out_ref):
    cols = pl.ds(pl.multiple_of(pl.program_id(0) * tile, tile), tile)
    total = gram_ref[cols, :]
    for i in range(2):
        total += lax.dot_general(
            wl_ref[i, :, cols], wr_ref[i], (((0,), (0,)), ((), ())), preferred_element_type=jnp.float32
        )
    out_ref[...] = total * scale


def on_device(ne, nc, partials, gaps, arc_start, taps):
    rows, width = partials.shape
    rwidth = width * nc // ne
    lags = jnp.pad(taps.astype(jnp.float32), (rows, rows - taps.shape[0]))[None, :]
    hbm, vmem = pl.BlockSpec(memory_space=pl.ANY), pl.BlockSpec(memory_space=pltpu.VMEM)
    gram, wl_last, wr_last = pl.pallas_call(
        functools.partial(kernel, ne, nc),
        out_shape=(
            pltpu.VMEM((width, rwidth), jnp.float32),
            pltpu.VMEM((2, rows, width), jnp.bfloat16),
            pltpu.VMEM((2, rows, rwidth), jnp.bfloat16),
        ),
        in_specs=[pl.BlockSpec(memory_space=pltpu.SMEM), hbm, hbm, hbm],
        out_specs=(vmem, vmem, vmem),
        scratch_shapes=[
            pltpu.VMEM((ne, rows, width), jnp.bfloat16),
            pltpu.VMEM((ne, rows, rwidth), jnp.bfloat16),
            pltpu.VMEM((rows, 2 * rows), jnp.float32),
            pltpu.VMEM((rows, width), jnp.bfloat16),
            pltpu.VMEM((rows, rwidth), jnp.bfloat16),
            pltpu.VMEM((1, rows), jnp.int32),
            pltpu.VMEM((1, 2 * rows), jnp.float32),
            pltpu.SemaphoreType.DMA((ne, CHUNKS)),
            pltpu.SemaphoreType.DMA((ne, CHUNKS)),
            pltpu.SemaphoreType.DMA((ne,)),
            pltpu.SemaphoreType.DMA((ne,)),
            pltpu.SemaphoreType.DMA((ne,)),
            pltpu.SemaphoreType.DMA((ne,)),
            pltpu.SemaphoreType.DMA((ne, nc // 2)),
            pltpu.SemaphoreType.DMA((nc // 2,)),
            pltpu.SemaphoreType.DMA((3,)),
        ],
        compiler_params=pltpu.CompilerParams(
            collective_id=0, has_side_effects=True, vmem_limit_bytes=48 * 1024 * 1024
        ),
        cost_estimate=pl.CostEstimate(
            flops=2 * ne * rows * width * rwidth, bytes_accessed=4 * width * rwidth, transcendentals=0
        ),
    )(arc_start, gaps[None, :], lags, partials)
    tile = min(256, width)
    return pl.pallas_call(
        functools.partial(finish, tile, (rows * ne) ** (-0.5)),
        out_shape=jax.ShapeDtypeStruct((width, rwidth), jnp.float32),
        grid=(width // tile,),
        in_specs=[vmem, vmem, vmem],
        out_specs=pl.BlockSpec((tile, rwidth), lambda i: (i, 0)),
        compiler_params=pltpu.CompilerParams(vmem_limit_bytes=16 * 1024 * 1024),
        cost_estimate=pl.CostEstimate(
            flops=4 * rows * width * rwidth, bytes_accessed=4 * width * rwidth, transcendentals=0
        ),
    )(gram, wl_last, wr_last)


def solution(mesh):
    in_specs = (P("epoch", "col"), P("epoch"), P(), P())
    out_specs = P("col", "epoch")
    ne, nc = mesh.shape["epoch"], mesh.shape["col"]
    return jax.shard_map(
        functools.partial(on_device, ne, nc),
        mesh=mesh, in_specs=in_specs, out_specs=out_specs, check_vma=False,
    )
```

```python
import functools

import jax
import jax.numpy as jnp
from jax import lax
from jax.experimental import pallas as pl
from jax.experimental.pallas import tpu as pltpu
from jax.sharding import PartitionSpec as P

MESH = pl.DeviceIdType.MESH
CHUNKS = 8


def kernel(
    ne, nc, arc_ref, gaps_ref, taps_ref, part_ref, out_ref, wl_last, wr_last,
    left, right, table, wl, wr, gaps_here, taps_here,
    left_recv, right_recv, up_send, dn_send, y_send, sib_send, x_send, x_last, in_sem,
):
    rows, width = part_ref.shape
    rwidth = right.shape[2]
    nz, nh = ne // 2, nc // 2
    G = CHUNKS
    crows = rows // G
    e, c = lax.axis_index("epoch"), lax.axis_index("col")
    z, y = e // 2, e % 2
    h, k = c // 2, c % 2
    src = e * nc // ne
    h_src, k_src = src // 2, src % 2
    offset = pl.multiple_of((e * nc % ne) // nc * rwidth, rwidth)
    is_src = c == src
    is_relay = jnp.logical_and(k == k_src, h != h_src)
    has_up, has_dn = z < nz - 1, z > 0
    up, dn, across, sib = e + 2, e - 2, e + 1 - 2 * y, c + 1 - 2 * k

    low, high = z == 0, z == nz - 1
    near_low, near_high = z == 1, z == nz - 2
    end, near = jnp.logical_or(low, high), jnp.logical_or(near_low, near_high)
    slabs = jnp.where(near, nz - 1, nz)
    far = jnp.where(z <= 1, nz - 1, 0)
    beside = jnp.where(z <= 1, 0, nz - 1)

    load_rows = pltpu.make_async_copy(part_ref, left.at[e], in_sem.at[0])
    load_gaps = pltpu.make_async_copy(gaps_ref, gaps_here, in_sem.at[1])
    load_taps = pltpu.make_async_copy(taps_ref, taps_here, in_sem.at[2])
    load_rows.start()
    load_gaps.start()
    load_taps.start()
    barrier = pltpu.get_barrier_semaphore()

    def greet(ee, cc):
        pl.semaphore_signal(barrier, inc=1, device_id=(ee, cc), device_id_type=MESH)

    @pl.when(has_up)
    def _():
        greet(up, c)

    @pl.when(has_dn)
    def _():
        greet(dn, c)

    greet(across, c)
    for i in range(1, nc):
        greet(e, lax.rem(c + i, nc))

    load_rows.wait()
    load_gaps.wait()
    load_taps.wait()
    eye = lax.broadcasted_iota(jnp.int32, (rows, rows), 0) == lax.broadcasted_iota(jnp.int32, (rows, rows), 1)
    column = jnp.sum(jnp.where(eye, gaps_here[...].astype(jnp.float32), 0.0), axis=1, keepdims=True)
    left[e] = left[e] * column.astype(jnp.bfloat16)

    pl.semaphore_wait(barrier, nc + has_up.astype(jnp.int32) + has_dn.astype(jnp.int32))

    def slab(t):
        both = 2 * jnp.minimum(z, nz - 1 - z)
        alternate = jnp.where(t % 2 == 1, z - (t + 1) // 2, z + t // 2)
        rest = jnp.where(z <= nz - 1 - z, t, nz - 1 - t)
        middle = jnp.where(t <= both, alternate, rest)
        return jnp.where(z <= 1, z + t, jnp.where(z >= nz - 2, z - t, middle))

    b_last = 2 * slab(slabs - 1) + 1 - y

    def piece(buf, b, g):
        return buf.at[b, pl.ds(pl.multiple_of(g * crows, crows), crows)]

    def send_left(b, g, sem, ee):
        pltpu.make_async_remote_copy(
            src_ref=piece(left, b, g), dst_ref=piece(left, b, g),
            send_sem=sem.at[b], recv_sem=left_recv.at[b, g],
            device_id=(ee, c), device_id_type=MESH,
        ).start()

    def right_source(b, g):
        return left.at[b, pl.ds(pl.multiple_of(g * crows, crows), crows), pl.ds(offset, rwidth)]

    def send_right(source, b, g, sem, cc):
        pltpu.make_async_remote_copy(
            src_ref=source, dst_ref=piece(right, b, g),
            send_sem=sem, recv_sem=right_recv.at[b, g],
            device_id=(e, cc), device_id_type=MESH,
        ).start()

    def spread(b, g):
        @pl.when(is_src)
        def _():
            pltpu.make_async_copy(right_source(b, g), piece(right, b, g), right_recv.at[b, g]).start()
            for i in range(1, nh):
                send_right(right_source(b, g), b, g, x_send.at[b, i - 1], lax.rem(h + i, nh) * 2 + k)
            send_right(right_source(b, g), b, g, sib_send.at[b], sib)

            @pl.when(b == b_last)
            def _():
                for i in range(1, nh):
                    send_right(right_source(b, g), b, g, x_last.at[i - 1], lax.rem(h + i, nh) * 2 + 1 - k)

    def wait_left(b, g):
        pltpu.make_async_copy(piece(left, b, g), piece(left, b, g), left_recv.at[b, g]).wait()

    def wait_right(b, g):
        pltpu.make_async_copy(piece(right, b, g), piece(right, b, g), right_recv.at[b, g]).wait()

        @pl.when(jnp.logical_and(is_relay, b != b_last))
        def _():
            send_right(piece(right, b, g), b, g, sib_send.at[b], sib)

    def own(g, carry):
        @pl.when(has_up)
        def _():
            send_left(e, g, up_send, up)

        @pl.when(has_dn)
        def _():
            send_left(e, g, dn_send, dn)

        send_left(e, g, y_send, across)
        spread(e, g)
        return carry

    lax.fori_loop(0, G, own, 0)

    lags = pltpu.roll(
        jnp.broadcast_to(taps_here[...], (2 * rows, 2 * rows)), 0, 1, stride=1, stride_axis=0
    )
    table[...] = lags[:, :rows].T
    out_ref[...] = jnp.zeros_like(out_ref)
    wl_last[rows:] = jnp.zeros((2 * rows, width), jnp.bfloat16)
    wr_last[rows:] = jnp.zeros((2 * rows, rwidth), jnp.bfloat16)

    def whiten_into(b, into_left, into_right):
        first = b * rows
        before = jnp.maximum(b - 1, 0)
        later = first + lax.broadcasted_iota(jnp.int32, (rows, 2 * rows), 0)
        source = first - rows + lax.broadcasted_iota(jnp.int32, (rows, 2 * rows), 1)
        boundary = arc_ref[0]
        same = (later >= boundary) == (source >= boundary)
        keep = jnp.logical_and(same, source >= 0)
        taps = jnp.where(keep, table[...], 0.0).astype(jnp.bfloat16)
        edge, inner = taps[:, :rows], taps[:, rows:]

        def whiten(buf, into, step):
            @pl.loop(0, into.shape[1] // step)
            def _(i):
                cols = pl.ds(pl.multiple_of(i * step, step), step)
                white = jnp.dot(inner, buf[b, :, cols], preferred_element_type=jnp.float32)
                white += jnp.dot(edge, buf[before, :, cols], preferred_element_type=jnp.float32)
                into[:, cols] = white.astype(jnp.bfloat16)

        whiten(left, into_left, min(512, width))
        whiten(right, into_right, min(512, rwidth))

    def add(blocks):
        depth = pl.ds(0, blocks * rows)

        @pl.loop(0, width // 256)
        def _(i):
            cols = pl.ds(pl.multiple_of(i * 256, 256), 256)
            out_ref[cols, :] += lax.dot_general(
                wl[depth, cols], wr[depth, :], (((0,), (0,)), ((), ())), preferred_element_type=jnp.float32
            )

    def part(buf, i):
        return buf.at[pl.ds(pl.multiple_of(i * rows, rows), rows)]

    def chunk(t, g):
        return jnp.where(jnp.logical_and(end, t == nz - 1), g % 2 * (G // 2) + g // 2, g)

    def step(it, carry):
        t, g = it // G, it % G
        moving = t < nz

        @pl.when(jnp.logical_and(moving, z - t - 1 >= 0))
        def _():
            b = e - 2 * (t + 1)
            wait_left(b, g)

            @pl.when(has_up)
            def _():
                send_left(b, g, up_send, up)

            spread(b, g)

        @pl.when(jnp.logical_and(moving, z + t + 1 < nz))
        def _():
            b = e + 2 * (t + 1)
            wait_left(b, g)

            @pl.when(has_dn)
            def _():
                send_left(b, g, dn_send, dn)

            spread(b, g)

        by_y = jnp.logical_or(t + 1 < nz - 1, jnp.logical_or(jnp.logical_not(end), g < G // 2))

        @pl.when(jnp.logical_and(t + 1 < slabs, by_y))
        def _():
            send_left(2 * slab(t + 1) + y, g, y_send, across)

        @pl.when(t < slabs)
        def _():
            b = 2 * slab(t) + 1 - y
            wait_left(b, chunk(t, g))
            to_near = jnp.logical_and(end, t == 0)
            to_end = jnp.logical_and(near, jnp.logical_and(t == nz - 2, g >= G // 2))

            @pl.when(jnp.logical_or(jnp.logical_and(low, to_near), jnp.logical_and(near_high, to_end)))
            def _():
                send_left(b, g, up_send, up)

            @pl.when(jnp.logical_or(jnp.logical_and(high, to_near), jnp.logical_and(near_low, to_end)))
            def _():
                send_left(b, g, dn_send, dn)

            spread(b, chunk(t, g))

        @pl.when(jnp.logical_and(near, t == 1))
        def _():
            b = 2 * beside + 1 - y
            wait_left(b, g)
            spread(b, g)

        @pl.when(t == 0)
        def _():
            wait_right(e, g)

        last = jnp.maximum(it - 1, 0)
        pt, pg = last // G, last % G
        passed = jnp.logical_and(it >= 1, pt < nz)

        @pl.when(jnp.logical_and(passed, z - pt - 1 >= 0))
        def _():
            wait_right(e - 2 * (pt + 1), pg)

        @pl.when(jnp.logical_and(passed, z + pt + 1 < nz))
        def _():
            wait_right(e + 2 * (pt + 1), pg)

        @pl.when(jnp.logical_and(it >= 1, pt < slabs))
        def _():
            wait_right(2 * slab(pt) + 1 - y, chunk(pt, pg))

        @pl.when(jnp.logical_and(it >= 1, jnp.logical_and(near, pt == 1)))
        def _():
            wait_right(2 * beside + 1 - y, pg)

        s = slab(jnp.clip(t - 1, 0, slabs - 1))
        s_now = slab(jnp.minimum(t, slabs - 1))
        below = s < z
        post_a = jnp.where(s > z, 2 * s + 1 - y, 2 * s + 1)
        post_b = jnp.where(
            s > z,
            2 * s + 1,
            jnp.where(jnp.logical_and(below, y == 0), 2 * s + 2, 0),
        )
        valid_b = jnp.where(
            s > z,
            y == 1,
            jnp.where(below, jnp.logical_or(y == 0, s == 0), s == 0),
        )
        pre = jnp.where(s_now > z, 2 * s_now, jnp.where(y == 0, 0, 2 * s_now + 2))
        valid_pre = jnp.where(
            s_now > z, y == 0, jnp.logical_and(s_now < z, jnp.logical_or(y == 1, s_now == 0))
        )
        quarter, on_quarter = g // (G // 4), g % (G // 4) == 0
        at0, at1, at2, at3 = quarter == 0, quarter == 1, quarter == 2, quarter == 3
        free = jnp.where(near_low == (y == 0), 1, 2)
        early = jnp.logical_and(t == 1, at3)
        middling = jnp.logical_and(t == 2, quarter == free)
        late = jnp.logical_and(t == 2, at3)
        first_low = jnp.where(y == 0, 0, 2)
        middling_low, late_low = jnp.where(y == 0, 2, 0), 1
        middling_high, late_high = ne - 2, ne - 1
        extra = jnp.where(
            near_low,
            jnp.where(early, first_low, jnp.where(late, late_low, middling_low)),
            jnp.where(jnp.logical_or(early, middling), middling_high, late_high),
        )
        valid_extra = jnp.where(
            near_low,
            jnp.logical_or(early, jnp.logical_or(middling, late)),
            jnp.logical_and(
                near_high,
                jnp.logical_or(late, jnp.where(y == 0, early, middling)),
            ),
        )
        valid_post = jnp.logical_and(
            jnp.logical_and(t >= 1, t <= slabs),
            jnp.logical_or(at0, jnp.logical_and(at1, valid_b)),
        )
        valid_pre = jnp.logical_and(jnp.logical_and(t >= 1, t < slabs), jnp.logical_and(at2, valid_pre))
        task = jnp.where(at0, post_a, jnp.where(at1, post_b, pre))
        task = jnp.where(valid_extra, extra, task)
        valid = jnp.logical_or(valid_extra, jnp.logical_or(valid_post, valid_pre))
        valid = jnp.logical_and(on_quarter, valid)

        held = jnp.logical_or(t == slabs, jnp.logical_and(valid_pre, t == slabs - 1))
        paired = jnp.logical_and(valid_post, valid_b)

        @pl.when(jnp.logical_and(valid, jnp.logical_not(held)))
        def _():
            second = jnp.logical_and(paired, at1).astype(jnp.int32)
            whiten_into(task, part(wl, second), part(wr, second))

            @pl.when(jnp.logical_not(paired))
            def _():
                add(1)

            @pl.when(jnp.logical_and(paired, at1))
            def _():
                add(2)

        @pl.when(jnp.logical_and(valid, held))
        def _():
            whiten_into(task, part(wl_last, quarter), part(wr_last, quarter))

        return carry

    lax.fori_loop(0, nz * G + G // 4 + 1, step, 0)

    def drain(b, carry):
        def sent(buf, sem, part=rows):
            span = buf.at[b, pl.ds(0, part)]
            pltpu.make_async_copy(span, span, sem).wait()

        mine = b % 2 == y
        whole_b = jnp.logical_and(end, b == e + 1 - 2 * y)
        half_b = jnp.logical_and(near, b == 2 * far + 1 - y)

        @pl.when(jnp.logical_or(jnp.logical_and(mine, jnp.logical_and(has_up, b <= e)), jnp.logical_and(low, whole_b)))
        def _():
            sent(left, up_send.at[b])

        @pl.when(jnp.logical_or(jnp.logical_and(mine, jnp.logical_and(has_dn, b >= e)), jnp.logical_and(high, whole_b)))
        def _():
            sent(left, dn_send.at[b])

        @pl.when(jnp.logical_and(near_high, half_b))
        def _():
            sent(left, up_send.at[b], rows // 2)

        @pl.when(jnp.logical_and(near_low, half_b))
        def _():
            sent(left, dn_send.at[b], rows // 2)

        halved = jnp.logical_and(end, b == 2 * far + y)
        skipped = jnp.logical_and(near, b == 2 * beside + y)

        @pl.when(jnp.logical_and(mine, jnp.logical_not(jnp.logical_or(halved, skipped))))
        def _():
            sent(left, y_send.at[b])

        @pl.when(halved)
        def _():
            sent(left, y_send.at[b], rows // 2)

        @pl.when(is_src)
        def _():
            for i in range(1, nh):
                sent(right, x_send.at[b, i - 1])

        @pl.when(jnp.logical_or(is_src, jnp.logical_and(is_relay, b != b_last)))
        def _():
            sent(right, sib_send.at[b])

        @pl.when(jnp.logical_and(is_src, b == b_last))
        def _():
            for i in range(1, nh):
                sent(right, x_last.at[i - 1])

        return carry

    lax.fori_loop(0, ne, drain, 0)


def finish(tile, scale, gram_ref, wl_ref, wr_ref, out_ref, buf, sem):
    tiles = gram_ref.shape[0] // tile

    def write(i):
        cols = pl.ds(pl.multiple_of(i * tile, tile), tile)
        return pltpu.make_async_copy(buf.at[cols], out_ref.at[cols], sem.at[i])

    @pl.loop(0, tiles)
    def _(i):
        cols = pl.ds(pl.multiple_of(i * tile, tile), tile)
        product = lax.dot_general(
            wl_ref[:, cols], wr_ref[...], (((0,), (0,)), ((), ())), preferred_element_type=jnp.float32
        )
        buf[cols, :] = (gram_ref[cols, :] + product) * scale
        write(i).start()

    @pl.loop(0, tiles)
    def _(i):
        write(i).wait()


def on_device(ne, nc, partials, gaps, arc_start, taps):
    rows, width = partials.shape
    rwidth = width * nc // ne
    lags = jnp.pad(taps.astype(jnp.float32), (rows, rows - taps.shape[0]))[None, :]
    hbm, vmem = pl.BlockSpec(memory_space=pl.ANY), pl.BlockSpec(memory_space=pltpu.VMEM)
    gram, wl_last, wr_last = pl.pallas_call(
        functools.partial(kernel, ne, nc),
        out_shape=(
            pltpu.VMEM((width, rwidth), jnp.float32),
            pltpu.VMEM((3 * rows, width), jnp.bfloat16),
            pltpu.VMEM((3 * rows, rwidth), jnp.bfloat16),
        ),
        in_specs=[pl.BlockSpec(memory_space=pltpu.SMEM), hbm, hbm, hbm],
        out_specs=(vmem, vmem, vmem),
        scratch_shapes=[
            pltpu.VMEM((ne, rows, width), jnp.bfloat16),
            pltpu.VMEM((ne, rows, rwidth), jnp.bfloat16),
            pltpu.VMEM((rows, 2 * rows), jnp.float32),
            pltpu.VMEM((2 * rows, width), jnp.bfloat16),
            pltpu.VMEM((2 * rows, rwidth), jnp.bfloat16),
            pltpu.VMEM((1, rows), jnp.int32),
            pltpu.VMEM((1, 2 * rows), jnp.float32),
            pltpu.SemaphoreType.DMA((ne, CHUNKS)),
            pltpu.SemaphoreType.DMA((ne, CHUNKS)),
            pltpu.SemaphoreType.DMA((ne,)),
            pltpu.SemaphoreType.DMA((ne,)),
            pltpu.SemaphoreType.DMA((ne,)),
            pltpu.SemaphoreType.DMA((ne,)),
            pltpu.SemaphoreType.DMA((ne, nc // 2)),
            pltpu.SemaphoreType.DMA((nc // 2,)),
            pltpu.SemaphoreType.DMA((3,)),
        ],
        compiler_params=pltpu.CompilerParams(
            collective_id=0, has_side_effects=True, vmem_limit_bytes=44 * 1024 * 1024
        ),
        cost_estimate=pl.CostEstimate(
            flops=2 * ne * rows * width * rwidth, bytes_accessed=4 * width * rwidth, transcendentals=0
        ),
    )(arc_start, gaps[None, :], lags, partials)
    tile = min(256, width)
    return pl.pallas_call(
        functools.partial(finish, tile, (rows * ne) ** (-0.5)),
        out_shape=jax.ShapeDtypeStruct((width, rwidth), jnp.float32),
        in_specs=[vmem, vmem, vmem],
        out_specs=hbm,
        scratch_shapes=[
            pltpu.VMEM((width, rwidth), jnp.float32),
            pltpu.SemaphoreType.DMA((width // tile,)),
        ],
        compiler_params=pltpu.CompilerParams(vmem_limit_bytes=24 * 1024 * 1024),
        cost_estimate=pl.CostEstimate(
            flops=4 * rows * width * rwidth, bytes_accessed=4 * width * rwidth, transcendentals=0
        ),
    )(gram, wl_last, wr_last)


def solution(mesh):
    in_specs = (P("epoch", "col"), P("epoch"), P(), P())
    out_specs = P("col", "epoch")
    ne, nc = mesh.shape["epoch"], mesh.shape["col"]
    return jax.shard_map(
        functools.partial(on_device, ne, nc),
        mesh=mesh, in_specs=in_specs, out_specs=out_specs, check_vma=False,
    )
```

```python
import functools

import jax
import jax.numpy as jnp
from jax import lax
from jax.experimental import pallas as pl
from jax.experimental.pallas import tpu as pltpu
from jax.sharding import PartitionSpec as P

MESH = pl.DeviceIdType.MESH
CHUNKS = 8


def kernel(
    ne, nc, arc_ref, gaps_ref, taps_ref, part_ref, out_ref, wl_last, wr_last,
    left, right, table, wl, wr, gaps_here, taps_here,
    left_recv, right_recv, up_send, dn_send, y_send, sib_send, x_send, x_last, in_sem,
):
    rows, width = part_ref.shape
    rwidth = right.shape[2]
    nz, nh = ne // 2, nc // 2
    G = CHUNKS
    crows = rows // G
    e, c = lax.axis_index("epoch"), lax.axis_index("col")
    z, y = e // 2, e % 2
    h, k = c // 2, c % 2
    src = e * nc // ne
    h_src, k_src = src // 2, src % 2
    offset = pl.multiple_of((e * nc % ne) // nc * rwidth, rwidth)
    is_src = c == src
    is_relay = jnp.logical_and(k == k_src, h != h_src)
    has_up, has_dn = z < nz - 1, z > 0
    up, dn, across, sib = e + 2, e - 2, e + 1 - 2 * y, c + 1 - 2 * k

    low, high = z == 0, z == nz - 1
    near_low, near_high = z == 1, z == nz - 2
    end, near = jnp.logical_or(low, high), jnp.logical_or(near_low, near_high)
    slabs = jnp.where(near, nz - 1, nz)
    far = jnp.where(z <= 1, nz - 1, 0)
    beside = jnp.where(z <= 1, 0, nz - 1)

    load_rows = pltpu.make_async_copy(part_ref, left.at[e], in_sem.at[0])
    load_gaps = pltpu.make_async_copy(gaps_ref, gaps_here, in_sem.at[1])
    load_taps = pltpu.make_async_copy(taps_ref, taps_here, in_sem.at[2])
    load_rows.start()
    load_gaps.start()
    load_taps.start()
    barrier = pltpu.get_barrier_semaphore()

    def greet(ee, cc):
        pl.semaphore_signal(barrier, inc=1, device_id=(ee, cc), device_id_type=MESH)

    @pl.when(has_up)
    def _():
        greet(up, c)

    @pl.when(has_dn)
    def _():
        greet(dn, c)

    greet(across, c)
    for i in range(1, nc):
        greet(e, lax.rem(c + i, nc))

    load_rows.wait()
    load_gaps.wait()
    load_taps.wait()
    eye = lax.broadcasted_iota(jnp.int32, (rows, rows), 0) == lax.broadcasted_iota(jnp.int32, (rows, rows), 1)
    column = jnp.sum(jnp.where(eye, gaps_here[...].astype(jnp.float32), 0.0), axis=1, keepdims=True)
    left[e] = left[e] * column.astype(jnp.bfloat16)

    pl.semaphore_wait(barrier, nc + has_up.astype(jnp.int32) + has_dn.astype(jnp.int32))

    def slab(t):
        both = 2 * jnp.minimum(z, nz - 1 - z)
        alternate = jnp.where(t % 2 == 1, z - (t + 1) // 2, z + t // 2)
        rest = jnp.where(z <= nz - 1 - z, t, nz - 1 - t)
        middle = jnp.where(t <= both, alternate, rest)
        return jnp.where(z <= 1, z + t, jnp.where(z >= nz - 2, z - t, middle))

    b_last = 2 * slab(slabs - 1) + 1 - y

    def piece(buf, b, g):
        return buf.at[b, pl.ds(pl.multiple_of(g * crows, crows), crows)]

    halves = 2 * rwidth == width
    groups = G // 4

    def last_rows(i):
        if not halves:
            return pl.ds(pl.multiple_of(i * crows, crows), crows)
        group = i // (G // 2) * groups + i % groups
        return pl.ds(pl.multiple_of(group * 2 * crows, 2 * crows), 2 * crows)

    def last_piece(b, i, ee):
        if not halves:
            return left.at[b, last_rows(i)]
        second = (i % (G // 2) // groups + ee * nc % ne // nc) % 2
        return left.at[b, last_rows(i), pl.ds(pl.multiple_of(second * rwidth, rwidth), rwidth)]

    def last_spreads(i):
        return i % (G // 2) < groups if halves else i >= 0

    def send_last(b, i, sem, ee):
        pltpu.make_async_remote_copy(
            src_ref=last_piece(b, i, ee), dst_ref=last_piece(b, i, ee),
            send_sem=sem.at[b], recv_sem=left_recv.at[b, i],
            device_id=(ee, c), device_id_type=MESH,
        ).start()

    def spread_last(b, i):
        source = left.at[b, last_rows(i), pl.ds(offset, rwidth)]
        target = right.at[b, last_rows(i)]

        def send(sem, cc):
            pltpu.make_async_remote_copy(
                src_ref=source, dst_ref=target, send_sem=sem, recv_sem=right_recv.at[b, i],
                device_id=(e, cc), device_id_type=MESH,
            ).start()

        @pl.when(jnp.logical_and(is_src, last_spreads(i)))
        def _():
            for n in range(1, nh):
                send(x_send.at[b, n - 1], lax.rem(h + n, nh) * 2 + k)
                send(x_last.at[n - 1], lax.rem(h + n, nh) * 2 + 1 - k)
            send(sib_send.at[b], sib)
            pltpu.make_async_copy(source, target, right_recv.at[b, i]).start()

    def send_left(b, g, sem, ee):
        pltpu.make_async_remote_copy(
            src_ref=piece(left, b, g), dst_ref=piece(left, b, g),
            send_sem=sem.at[b], recv_sem=left_recv.at[b, g],
            device_id=(ee, c), device_id_type=MESH,
        ).start()

    def right_source(b, g):
        return left.at[b, pl.ds(pl.multiple_of(g * crows, crows), crows), pl.ds(offset, rwidth)]

    def send_right(source, b, g, sem, cc):
        pltpu.make_async_remote_copy(
            src_ref=source, dst_ref=piece(right, b, g),
            send_sem=sem, recv_sem=right_recv.at[b, g],
            device_id=(e, cc), device_id_type=MESH,
        ).start()

    def spread(b, g):
        @pl.when(is_src)
        def _():
            pltpu.make_async_copy(right_source(b, g), piece(right, b, g), right_recv.at[b, g]).start()
            for i in range(1, nh):
                send_right(right_source(b, g), b, g, x_send.at[b, i - 1], lax.rem(h + i, nh) * 2 + k)
            send_right(right_source(b, g), b, g, sib_send.at[b], sib)

            @pl.when(b == b_last)
            def _():
                for i in range(1, nh):
                    send_right(right_source(b, g), b, g, x_last.at[i - 1], lax.rem(h + i, nh) * 2 + 1 - k)

    def wait_left(b, g):
        pltpu.make_async_copy(piece(left, b, g), piece(left, b, g), left_recv.at[b, g]).wait()

    def wait_right(b, g):
        pltpu.make_async_copy(piece(right, b, g), piece(right, b, g), right_recv.at[b, g]).wait()

        @pl.when(jnp.logical_and(is_relay, b != b_last))
        def _():
            send_right(piece(right, b, g), b, g, sib_send.at[b], sib)

    def own(g, carry):
        @pl.when(has_up)
        def _():
            send_left(e, g, up_send, up)

        @pl.when(has_dn)
        def _():
            send_left(e, g, dn_send, dn)

        send_left(e, g, y_send, across)
        spread(e, g)
        return carry

    lax.fori_loop(0, G, own, 0)

    lags = pltpu.roll(
        jnp.broadcast_to(taps_here[...], (2 * rows, 2 * rows)), 0, 1, stride=1, stride_axis=0
    )
    table[...] = lags[:, :rows].T
    out_ref[...] = jnp.zeros_like(out_ref)
    wl_last[rows:] = jnp.zeros((2 * rows, width), jnp.bfloat16)
    wr_last[rows:] = jnp.zeros((2 * rows, rwidth), jnp.bfloat16)

    def whiten_into(b, into_left, into_right):
        first = b * rows
        before = jnp.maximum(b - 1, 0)
        later = first + lax.broadcasted_iota(jnp.int32, (rows, 2 * rows), 0)
        source = first - rows + lax.broadcasted_iota(jnp.int32, (rows, 2 * rows), 1)
        boundary = arc_ref[0]
        same = (later >= boundary) == (source >= boundary)
        keep = jnp.logical_and(same, source >= 0)
        taps = jnp.where(keep, table[...], 0.0).astype(jnp.bfloat16)
        edge, inner = taps[:, :rows], taps[:, rows:]

        def whiten(buf, into, step):
            @pl.loop(0, into.shape[1] // step)
            def _(i):
                cols = pl.ds(pl.multiple_of(i * step, step), step)
                white = jnp.dot(inner, buf[b, :, cols], preferred_element_type=jnp.float32)
                white += jnp.dot(edge, buf[before, :, cols], preferred_element_type=jnp.float32)
                into[:, cols] = white.astype(jnp.bfloat16)

        whiten(left, into_left, min(512, width))
        whiten(right, into_right, min(512, rwidth))

    def add(blocks):
        depth = pl.ds(0, blocks * rows)

        @pl.loop(0, width // 256)
        def _(i):
            cols = pl.ds(pl.multiple_of(i * 256, 256), 256)
            out_ref[cols, :] += lax.dot_general(
                wl[depth, cols], wr[depth, :], (((0,), (0,)), ((), ())), preferred_element_type=jnp.float32
            )

    def part(buf, i):
        return buf.at[pl.ds(pl.multiple_of(i * rows, rows), rows)]

    def chunk(t, g):
        side = g % 2 * (G // 2) + g // 2
        turned = (g + G // 2) % G
        ends_last = jnp.logical_and(end, t == nz - 1)
        return jnp.where(ends_last, side, jnp.where(jnp.logical_and(near, t == nz - 2), turned, g))

    def step(it, carry):
        t, g = it // G, it % G
        moving = t < nz

        @pl.when(jnp.logical_and(moving, z - t - 1 >= 0))
        def _():
            b = e - 2 * (t + 1)
            wait_left(b, g)

            @pl.when(has_up)
            def _():
                send_left(b, g, up_send, up)

            spread(b, g)

        @pl.when(jnp.logical_and(moving, z + t + 1 < nz))
        def _():
            b = e + 2 * (t + 1)
            wait_left(b, g)

            @pl.when(has_dn)
            def _():
                send_left(b, g, dn_send, dn)

            spread(b, g)

        half = G // 2
        ends_next = jnp.logical_and(end, t + 1 == nz - 1)
        near_next = jnp.logical_and(near, t + 1 == nz - 2)
        near_last = jnp.logical_and(near, t == nz - 2)

        @pl.when(jnp.logical_or(
            jnp.logical_and(
                t + 1 < slabs,
                jnp.logical_not(jnp.logical_or(ends_next, jnp.logical_and(near_next, g < half))),
            ),
            jnp.logical_and(near_last, g < half),
        ))
        def _():
            send_left(2 * slab(jnp.minimum(t + 1, slabs - 1)) + y, g, y_send, across)

        @pl.when(jnp.logical_and(ends_next, g == half - 1))
        def _():
            for i in range(half):
                send_last(2 * far + y, i, y_send, across)

        ends_last = jnp.logical_and(end, t == nz - 1)

        @pl.when(ends_last)
        def _():
            i = chunk(t, g)
            piece_here = last_piece(b_last, i, e)
            pltpu.make_async_copy(piece_here, piece_here, left_recv.at[b_last, i]).wait()
            spread_last(b_last, i)

        @pl.when(jnp.logical_and(t < slabs, jnp.logical_not(ends_last)))
        def _():
            b = 2 * slab(t) + 1 - y
            wait_left(b, chunk(t, g))
            to_near = jnp.logical_and(end, t == 0)
            to_end = jnp.logical_and(near_last, g == half - 1)

            @pl.when(jnp.logical_and(low, to_near))
            def _():
                send_left(b, g, up_send, up)

            @pl.when(jnp.logical_and(high, to_near))
            def _():
                send_left(b, g, dn_send, dn)

            @pl.when(jnp.logical_and(near_high, to_end))
            def _():
                for i in range(half, G):
                    send_last(b, i, up_send, up)

            @pl.when(jnp.logical_and(near_low, to_end))
            def _():
                for i in range(half, G):
                    send_last(b, i, dn_send, dn)

            spread(b, chunk(t, g))

        @pl.when(jnp.logical_and(near, t == 1))
        def _():
            b = 2 * beside + 1 - y
            wait_left(b, g)
            spread(b, g)

        @pl.when(t == 0)
        def _():
            wait_right(e, g)

        last = jnp.maximum(it - 1, 0)
        pt, pg = last // G, last % G
        passed = jnp.logical_and(it >= 1, pt < nz)

        @pl.when(jnp.logical_and(passed, z - pt - 1 >= 0))
        def _():
            wait_right(e - 2 * (pt + 1), pg)

        @pl.when(jnp.logical_and(passed, z + pt + 1 < nz))
        def _():
            wait_right(e + 2 * (pt + 1), pg)

        ends_past = jnp.logical_and(end, pt == nz - 1)

        @pl.when(jnp.logical_and(it >= 1, jnp.logical_and(pt < slabs, jnp.logical_not(ends_past))))
        def _():
            wait_right(2 * slab(pt) + 1 - y, chunk(pt, pg))

        @pl.when(jnp.logical_and(ends_past, last_spreads(chunk(pt, pg))))
        def _():
            i = chunk(pt, pg)
            rows_here = right.at[b_last, last_rows(i)]
            pltpu.make_async_copy(rows_here, rows_here, right_recv.at[b_last, i]).wait()

        @pl.when(jnp.logical_and(it >= 1, jnp.logical_and(near, pt == 1)))
        def _():
            wait_right(2 * beside + 1 - y, pg)

        s = slab(jnp.clip(t - 1, 0, slabs - 1))
        s_now = slab(jnp.minimum(t, slabs - 1))
        below = s < z
        post_a = jnp.where(s > z, 2 * s + 1 - y, 2 * s + 1)
        post_b = jnp.where(
            s > z,
            2 * s + 1,
            jnp.where(jnp.logical_and(below, y == 0), 2 * s + 2, 0),
        )
        valid_b = jnp.where(
            s > z,
            y == 1,
            jnp.where(below, jnp.logical_or(y == 0, s == 0), s == 0),
        )
        pre = jnp.where(s_now > z, 2 * s_now, jnp.where(y == 0, 0, 2 * s_now + 2))
        valid_pre = jnp.where(
            s_now > z, y == 0, jnp.logical_and(s_now < z, jnp.logical_or(y == 1, s_now == 0))
        )
        quarter, on_quarter = g // (G // 4), g % (G // 4) == 0
        at0, at1, at2, at3 = quarter == 0, quarter == 1, quarter == 2, quarter == 3
        free = jnp.where(near_low == (y == 0), 1, 2)
        early = jnp.logical_and(t == 1, at3)
        middling = jnp.logical_and(t == 2, quarter == free)
        late = jnp.logical_and(t == 2, at3)
        first_low = jnp.where(y == 0, 0, 2)
        middling_low, late_low = jnp.where(y == 0, 2, 0), 1
        middling_high, late_high = ne - 2, ne - 1
        extra = jnp.where(
            near_low,
            jnp.where(early, first_low, jnp.where(late, late_low, middling_low)),
            jnp.where(jnp.logical_or(early, middling), middling_high, late_high),
        )
        valid_extra = jnp.where(
            near_low,
            jnp.logical_or(early, jnp.logical_or(middling, late)),
            jnp.logical_and(
                near_high,
                jnp.logical_or(late, jnp.where(y == 0, early, middling)),
            ),
        )
        valid_post = jnp.logical_and(
            jnp.logical_and(t >= 1, t <= slabs),
            jnp.logical_or(at0, jnp.logical_and(at1, valid_b)),
        )
        valid_pre = jnp.logical_and(jnp.logical_and(t >= 1, t < slabs), jnp.logical_and(at2, valid_pre))
        task = jnp.where(at0, post_a, jnp.where(at1, post_b, pre))
        task = jnp.where(valid_extra, extra, task)
        valid = jnp.logical_or(valid_extra, jnp.logical_or(valid_post, valid_pre))
        valid = jnp.logical_and(on_quarter, valid)

        held = jnp.logical_or(t == slabs, jnp.logical_and(valid_pre, t == slabs - 1))
        paired = jnp.logical_and(valid_post, valid_b)

        @pl.when(jnp.logical_and(valid, jnp.logical_not(held)))
        def _():
            second = jnp.logical_and(paired, at1).astype(jnp.int32)
            whiten_into(task, part(wl, second), part(wr, second))

            @pl.when(jnp.logical_not(paired))
            def _():
                add(1)

            @pl.when(jnp.logical_and(paired, at1))
            def _():
                add(2)

        @pl.when(jnp.logical_and(valid, held))
        def _():
            whiten_into(task, part(wl_last, quarter), part(wr_last, quarter))

        return carry

    lax.fori_loop(0, nz * G + G // 4 + 1, step, 0)

    def drain(b, carry):
        def sent(buf, sem, part=rows):
            span = buf.at[b, pl.ds(0, part)]
            pltpu.make_async_copy(span, span, sem).wait()

        mine = b % 2 == y
        whole_b = jnp.logical_and(end, b == e + 1 - 2 * y)
        half_b = jnp.logical_and(near, b == 2 * far + 1 - y)

        @pl.when(jnp.logical_or(jnp.logical_and(mine, jnp.logical_and(has_up, b <= e)), jnp.logical_and(low, whole_b)))
        def _():
            sent(left, up_send.at[b])

        @pl.when(jnp.logical_or(jnp.logical_and(mine, jnp.logical_and(has_dn, b >= e)), jnp.logical_and(high, whole_b)))
        def _():
            sent(left, dn_send.at[b])

        @pl.when(jnp.logical_and(near_high, half_b))
        def _():
            sent(left, up_send.at[b], rows // 2)

        @pl.when(jnp.logical_and(near_low, half_b))
        def _():
            sent(left, dn_send.at[b], rows // 2)

        halved = jnp.logical_and(end, b == 2 * far + y)
        skipped = jnp.logical_and(near, b == 2 * beside + y)

        @pl.when(jnp.logical_and(mine, jnp.logical_not(jnp.logical_or(halved, skipped))))
        def _():
            sent(left, y_send.at[b])

        @pl.when(halved)
        def _():
            sent(left, y_send.at[b], rows // 2)

        @pl.when(is_src)
        def _():
            for i in range(1, nh):
                sent(right, x_send.at[b, i - 1])

        @pl.when(jnp.logical_or(is_src, jnp.logical_and(is_relay, b != b_last)))
        def _():
            sent(right, sib_send.at[b])

        @pl.when(jnp.logical_and(is_src, b == b_last))
        def _():
            for i in range(1, nh):
                sent(right, x_last.at[i - 1])

        return carry

    lax.fori_loop(0, ne, drain, 0)


def finish(tile, scale, gram_ref, wl_ref, wr_ref, out_ref, buf, sem):
    tiles = gram_ref.shape[0] // tile

    def write(i):
        cols = pl.ds(pl.multiple_of(i * tile, tile), tile)
        return pltpu.make_async_copy(buf.at[cols], out_ref.at[cols], sem.at[i])

    @pl.loop(0, tiles)
    def _(i):
        cols = pl.ds(pl.multiple_of(i * tile, tile), tile)
        product = lax.dot_general(
            wl_ref[:, cols], wr_ref[...], (((0,), (0,)), ((), ())), preferred_element_type=jnp.float32
        )
        buf[cols, :] = (gram_ref[cols, :] + product) * scale
        write(i).start()

    @pl.loop(0, tiles)
    def _(i):
        write(i).wait()


def on_device(ne, nc, partials, gaps, arc_start, taps):
    rows, width = partials.shape
    rwidth = width * nc // ne
    lags = jnp.pad(taps.astype(jnp.float32), (rows, rows - taps.shape[0]))[None, :]
    hbm, vmem = pl.BlockSpec(memory_space=pl.ANY), pl.BlockSpec(memory_space=pltpu.VMEM)
    gram, wl_last, wr_last = pl.pallas_call(
        functools.partial(kernel, ne, nc),
        out_shape=(
            pltpu.VMEM((width, rwidth), jnp.float32),
            pltpu.VMEM((3 * rows, width), jnp.bfloat16),
            pltpu.VMEM((3 * rows, rwidth), jnp.bfloat16),
        ),
        in_specs=[pl.BlockSpec(memory_space=pltpu.SMEM), hbm, hbm, hbm],
        out_specs=(vmem, vmem, vmem),
        scratch_shapes=[
            pltpu.VMEM((ne, rows, width), jnp.bfloat16),
            pltpu.VMEM((ne, rows, rwidth), jnp.bfloat16),
            pltpu.VMEM((rows, 2 * rows), jnp.float32),
            pltpu.VMEM((2 * rows, width), jnp.bfloat16),
            pltpu.VMEM((2 * rows, rwidth), jnp.bfloat16),
            pltpu.VMEM((1, rows), jnp.int32),
            pltpu.VMEM((1, 2 * rows), jnp.float32),
            pltpu.SemaphoreType.DMA((ne, CHUNKS)),
            pltpu.SemaphoreType.DMA((ne, CHUNKS)),
            pltpu.SemaphoreType.DMA((ne,)),
            pltpu.SemaphoreType.DMA((ne,)),
            pltpu.SemaphoreType.DMA((ne,)),
            pltpu.SemaphoreType.DMA((ne,)),
            pltpu.SemaphoreType.DMA((ne, nc // 2)),
            pltpu.SemaphoreType.DMA((nc // 2,)),
            pltpu.SemaphoreType.DMA((3,)),
        ],
        compiler_params=pltpu.CompilerParams(
            collective_id=0, has_side_effects=True, vmem_limit_bytes=44 * 1024 * 1024
        ),
        cost_estimate=pl.CostEstimate(
            flops=2 * ne * rows * width * rwidth, bytes_accessed=4 * width * rwidth, transcendentals=0
        ),
    )(arc_start, gaps[None, :], lags, partials)
    tile = min(256, width)
    return pl.pallas_call(
        functools.partial(finish, tile, (rows * ne) ** (-0.5)),
        out_shape=jax.ShapeDtypeStruct((width, rwidth), jnp.float32),
        in_specs=[vmem, vmem, vmem],
        out_specs=hbm,
        scratch_shapes=[
            pltpu.VMEM((width, rwidth), jnp.float32),
            pltpu.SemaphoreType.DMA((width // tile,)),
        ],
        compiler_params=pltpu.CompilerParams(vmem_limit_bytes=24 * 1024 * 1024),
        cost_estimate=pl.CostEstimate(
            flops=4 * rows * width * rwidth, bytes_accessed=4 * width * rwidth, transcendentals=0
        ),
    )(gram, wl_last, wr_last)


def solution(mesh):
    in_specs = (P("epoch", "col"), P("epoch"), P(), P())
    out_specs = P("col", "epoch")
    ne, nc = mesh.shape["epoch"], mesh.shape["col"]
    return jax.shard_map(
        functools.partial(on_device, ne, nc),
        mesh=mesh, in_specs=in_specs, out_specs=out_specs, check_vma=False,
    )
```

```python
import functools

import jax
import jax.numpy as jnp
from jax import lax
from jax.experimental import pallas as pl
from jax.experimental.pallas import tpu as pltpu
from jax.sharding import PartitionSpec as P

MESH = pl.DeviceIdType.MESH
CHUNKS = 8


def kernel(
    ne, nc, arc_ref, gaps_ref, taps_ref, part_ref, out_ref, wl_last, wr_last,
    left_all, right_all, table, wl, wr, gaps_here, taps_here,
    left_recv, right_recv, up_send, dn_send, y_send, sib_send, x_send, in_sem,
):
    rows, width = part_ref.shape
    rwidth = right_all.shape[2]
    nz, nh = ne // 2, nc // 2
    left, right = left_all.at[pl.ds(1, ne)], right_all.at[pl.ds(1, ne)]
    G = CHUNKS
    crows = rows // G
    e, c = lax.axis_index("epoch"), lax.axis_index("col")
    z, y = e // 2, e % 2
    h, k = c // 2, c % 2
    src = e * nc // ne
    h_src, k_src = src // 2, src % 2
    offset = pl.multiple_of((e * nc % ne) // nc * rwidth, rwidth)
    is_src = c == src
    is_relay = jnp.logical_and(k == k_src, h != h_src)
    has_up, has_dn = z < nz - 1, z > 0
    up, dn, across, sib = e + 2, e - 2, e + 1 - 2 * y, c + 1 - 2 * k

    low, high = z == 0, z == nz - 1
    near_low, near_high = z == 1, z == nz - 2
    end, near = jnp.logical_or(low, high), jnp.logical_or(near_low, near_high)
    slabs = jnp.where(near, nz - 1, nz)
    far = jnp.where(z <= 1, nz - 1, 0)
    beside = jnp.where(z <= 1, 0, nz - 1)

    load_rows = pltpu.make_async_copy(part_ref, left.at[e], in_sem.at[0])
    load_gaps = pltpu.make_async_copy(gaps_ref, gaps_here, in_sem.at[1])
    load_taps = pltpu.make_async_copy(taps_ref, taps_here, in_sem.at[2])
    load_rows.start()
    load_gaps.start()
    load_taps.start()
    barrier = pltpu.get_barrier_semaphore()

    def greet(ee, cc):
        pl.semaphore_signal(barrier, inc=1, device_id=(ee, cc), device_id_type=MESH)

    @pl.when(has_up)
    def _():
        greet(up, c)

    @pl.when(has_dn)
    def _():
        greet(dn, c)

    greet(across, c)
    for i in range(1, nc):
        greet(e, lax.rem(c + i, nc))

    load_rows.wait()
    load_gaps.wait()
    load_taps.wait()
    eye = lax.broadcasted_iota(jnp.int32, (rows, rows), 0) == lax.broadcasted_iota(jnp.int32, (rows, rows), 1)
    column = jnp.sum(jnp.where(eye, gaps_here[...].astype(jnp.float32), 0.0), axis=1, keepdims=True)
    left[e] = left[e] * column.astype(jnp.bfloat16)

    pl.semaphore_wait(barrier, nc + has_up.astype(jnp.int32) + has_dn.astype(jnp.int32))

    def slab(t):
        both = 2 * jnp.minimum(z, nz - 1 - z)
        alternate = jnp.where(t % 2 == 1, z - (t + 1) // 2, z + t // 2)
        rest = jnp.where(z <= nz - 1 - z, t, nz - 1 - t)
        middle = jnp.where(t <= both, alternate, rest)
        return jnp.where(z <= 1, z + t, jnp.where(z >= nz - 2, z - t, middle))

    b_last = 2 * slab(slabs - 1) + 1 - y

    def piece(buf, b, g):
        return buf.at[b, pl.ds(pl.multiple_of(g * crows, crows), crows)]

    halves = 2 * rwidth == width
    groups = G // 4

    def last_rows(i):
        if not halves:
            return pl.ds(pl.multiple_of(i * crows, crows), crows)
        group = i // (G // 2) * groups + i % groups
        return pl.ds(pl.multiple_of(group * 2 * crows, 2 * crows), 2 * crows)

    def last_piece(b, i, ee):
        if not halves:
            return left.at[b, last_rows(i)]
        second = (i % (G // 2) // groups + ee * nc % ne // nc) % 2
        return left.at[b, last_rows(i), pl.ds(pl.multiple_of(second * rwidth, rwidth), rwidth)]

    def last_spreads(i):
        return i % (G // 2) < groups if halves else i >= 0

    def send_last(b, i, sem, ee):
        pltpu.make_async_remote_copy(
            src_ref=last_piece(b, i, ee), dst_ref=last_piece(b, i, ee),
            send_sem=sem.at[b], recv_sem=left_recv.at[b, i],
            device_id=(ee, c), device_id_type=MESH,
        ).start()

    def spread_last(b, i):
        source = left.at[b, last_rows(i), pl.ds(offset, rwidth)]
        target = right.at[b, last_rows(i)]

        def send(sem, cc):
            pltpu.make_async_remote_copy(
                src_ref=source, dst_ref=target, send_sem=sem, recv_sem=right_recv.at[b, i],
                device_id=(e, cc), device_id_type=MESH,
            ).start()

        @pl.when(jnp.logical_and(is_src, last_spreads(i)))
        def _():
            for n in range(1, nh):
                send(x_send.at[b, n - 1], lax.rem(h + n, nh) * 2 + k)
            send(sib_send.at[b], sib)
            pltpu.make_async_copy(source, target, right_recv.at[b, i]).start()

    def send_left(b, g, sem, ee):
        pltpu.make_async_remote_copy(
            src_ref=piece(left, b, g), dst_ref=piece(left, b, g),
            send_sem=sem.at[b], recv_sem=left_recv.at[b, g],
            device_id=(ee, c), device_id_type=MESH,
        ).start()

    def right_source(b, g):
        return left.at[b, pl.ds(pl.multiple_of(g * crows, crows), crows), pl.ds(offset, rwidth)]

    def send_right(source, b, g, sem, cc):
        pltpu.make_async_remote_copy(
            src_ref=source, dst_ref=piece(right, b, g),
            send_sem=sem, recv_sem=right_recv.at[b, g],
            device_id=(e, cc), device_id_type=MESH,
        ).start()

    def spread(b, g):
        @pl.when(is_src)
        def _():
            pltpu.make_async_copy(right_source(b, g), piece(right, b, g), right_recv.at[b, g]).start()
            for i in range(1, nh):
                send_right(right_source(b, g), b, g, x_send.at[b, i - 1], lax.rem(h + i, nh) * 2 + k)
            send_right(right_source(b, g), b, g, sib_send.at[b], sib)

    def wait_left(b, g):
        pltpu.make_async_copy(piece(left, b, g), piece(left, b, g), left_recv.at[b, g]).wait()

    def wait_right(b, g):
        pltpu.make_async_copy(piece(right, b, g), piece(right, b, g), right_recv.at[b, g]).wait()

        @pl.when(is_relay)
        def _():
            send_right(piece(right, b, g), b, g, sib_send.at[b], sib)

    def own(g, carry):
        @pl.when(has_up)
        def _():
            send_left(e, g, up_send, up)

        @pl.when(has_dn)
        def _():
            send_left(e, g, dn_send, dn)

        send_left(e, g, y_send, across)
        spread(e, g)
        return carry

    lax.fori_loop(0, G, own, 0)

    lags = pltpu.roll(
        jnp.broadcast_to(taps_here[...], (2 * rows, 2 * rows)), 0, 1, stride=1, stride_axis=0
    )
    table[...] = lags[:, :rows].T
    left_all[0] = jnp.zeros((rows, width), jnp.bfloat16)
    right_all[0] = jnp.zeros((rows, rwidth), jnp.bfloat16)
    out_ref[...] = jnp.zeros_like(out_ref)
    wl_last[rows:] = jnp.zeros((2 * rows, width), jnp.bfloat16)
    wr_last[rows:] = jnp.zeros((2 * rows, rwidth), jnp.bfloat16)

    def whiten_into(b, into_left, into_right):
        first = b * rows
        later = first + lax.broadcasted_iota(jnp.int32, (rows, 2 * rows), 0)
        source = first - rows + lax.broadcasted_iota(jnp.int32, (rows, 2 * rows), 1)
        boundary = arc_ref[0]
        same = (later >= boundary) == (source >= boundary)
        keep = jnp.logical_and(same, source >= 0)
        taps = jnp.where(keep, table[...], 0.0).astype(jnp.bfloat16)

        def whiten(buf, into, step):
            @pl.loop(0, into.shape[1] // step)
            def _(i):
                cols = pl.ds(pl.multiple_of(i * step, step), step)
                both = buf[pl.ds(b, 2), :, cols].reshape(2 * rows, step)
                white = jnp.dot(taps, both, preferred_element_type=jnp.float32)
                into[:, cols] = white.astype(jnp.bfloat16)

        whiten(left_all, into_left, min(512, width))
        whiten(right_all, into_right, min(512, rwidth))

    def add(blocks):
        depth = pl.ds(0, blocks * rows)

        @pl.loop(0, width // 256)
        def _(i):
            cols = pl.ds(pl.multiple_of(i * 256, 256), 256)
            out_ref[cols, :] += lax.dot_general(
                wl[depth, cols], wr[depth, :], (((0,), (0,)), ((), ())), preferred_element_type=jnp.float32
            )

    def part(buf, i):
        return buf.at[pl.ds(pl.multiple_of(i * rows, rows), rows)]

    def chunk(t, g):
        side = g % 2 * (G // 2) + g // 2
        turned = (g + G // 2) % G
        ends_last = jnp.logical_and(end, t == nz - 1)
        return jnp.where(ends_last, side, jnp.where(jnp.logical_and(near, t == nz - 2), turned, g))

    def step(it, carry):
        t, g = it // G, it % G
        moving = t < nz

        @pl.when(jnp.logical_and(moving, z - t - 1 >= 0))
        def _():
            b = e - 2 * (t + 1)
            wait_left(b, g)

            @pl.when(has_up)
            def _():
                send_left(b, g, up_send, up)

            spread(b, g)

        @pl.when(jnp.logical_and(moving, z + t + 1 < nz))
        def _():
            b = e + 2 * (t + 1)
            wait_left(b, g)

            @pl.when(has_dn)
            def _():
                send_left(b, g, dn_send, dn)

            spread(b, g)

        half = G // 2
        ends_next = jnp.logical_and(end, t + 1 == nz - 1)
        near_next = jnp.logical_and(near, t + 1 == nz - 2)
        near_last = jnp.logical_and(near, t == nz - 2)

        @pl.when(jnp.logical_or(
            jnp.logical_and(
                t + 1 < slabs,
                jnp.logical_not(jnp.logical_or(ends_next, jnp.logical_and(near_next, g < half))),
            ),
            jnp.logical_and(near_last, g < half),
        ))
        def _():
            send_left(2 * slab(jnp.minimum(t + 1, slabs - 1)) + y, g, y_send, across)

        @pl.when(jnp.logical_and(ends_next, g == half - 1))
        def _():
            for i in range(half):
                send_last(2 * far + y, i, y_send, across)

        ends_last = jnp.logical_and(end, t == nz - 1)

        @pl.when(ends_last)
        def _():
            i = chunk(t, g)
            piece_here = last_piece(b_last, i, e)
            pltpu.make_async_copy(piece_here, piece_here, left_recv.at[b_last, i]).wait()
            spread_last(b_last, i)

        @pl.when(jnp.logical_and(t < slabs, jnp.logical_not(ends_last)))
        def _():
            b = 2 * slab(t) + 1 - y
            wait_left(b, chunk(t, g))
            to_near = jnp.logical_and(end, t == 0)
            to_end = jnp.logical_and(near_last, g == half - 1)

            @pl.when(jnp.logical_and(low, to_near))
            def _():
                send_left(b, g, up_send, up)

            @pl.when(jnp.logical_and(high, to_near))
            def _():
                send_left(b, g, dn_send, dn)

            @pl.when(jnp.logical_and(near_high, to_end))
            def _():
                for i in range(half, G):
                    send_last(b, i, up_send, up)

            @pl.when(jnp.logical_and(near_low, to_end))
            def _():
                for i in range(half, G):
                    send_last(b, i, dn_send, dn)

            spread(b, chunk(t, g))

        @pl.when(jnp.logical_and(near, t == 1))
        def _():
            b = 2 * beside + 1 - y
            wait_left(b, g)
            spread(b, g)

        @pl.when(t == 0)
        def _():
            wait_right(e, g)

        last = jnp.maximum(it - 1, 0)
        pt, pg = last // G, last % G
        passed = jnp.logical_and(it >= 1, pt < nz)

        @pl.when(jnp.logical_and(passed, z - pt - 1 >= 0))
        def _():
            wait_right(e - 2 * (pt + 1), pg)

        @pl.when(jnp.logical_and(passed, z + pt + 1 < nz))
        def _():
            wait_right(e + 2 * (pt + 1), pg)

        ends_past = jnp.logical_and(end, pt == nz - 1)

        @pl.when(jnp.logical_and(it >= 1, jnp.logical_and(pt < slabs, jnp.logical_not(ends_past))))
        def _():
            wait_right(2 * slab(pt) + 1 - y, chunk(pt, pg))

        @pl.when(jnp.logical_and(ends_past, last_spreads(chunk(pt, pg))))
        def _():
            i = chunk(pt, pg)
            rows_here = right.at[b_last, last_rows(i)]
            pltpu.make_async_copy(rows_here, rows_here, right_recv.at[b_last, i]).wait()

            @pl.when(is_relay)
            def _():
                pltpu.make_async_remote_copy(
                    src_ref=rows_here, dst_ref=rows_here,
                    send_sem=sib_send.at[b_last], recv_sem=right_recv.at[b_last, i],
                    device_id=(e, sib), device_id_type=MESH,
                ).start()

        @pl.when(jnp.logical_and(it >= 1, jnp.logical_and(near, pt == 1)))
        def _():
            wait_right(2 * beside + 1 - y, pg)

        s = slab(jnp.clip(t - 1, 0, slabs - 1))
        s_now = slab(jnp.minimum(t, slabs - 1))
        below = s < z
        post_a = jnp.where(s > z, 2 * s + 1 - y, 2 * s + 1)
        post_b = jnp.where(
            s > z,
            2 * s + 1,
            jnp.where(jnp.logical_and(below, y == 0), 2 * s + 2, 0),
        )
        valid_b = jnp.where(
            s > z,
            y == 1,
            jnp.where(below, jnp.logical_or(y == 0, s == 0), s == 0),
        )
        pre = jnp.where(s_now > z, 2 * s_now, jnp.where(y == 0, 0, 2 * s_now + 2))
        valid_pre = jnp.where(
            s_now > z, y == 0, jnp.logical_and(s_now < z, jnp.logical_or(y == 1, s_now == 0))
        )
        quarter, on_quarter = g // (G // 4), g % (G // 4) == 0
        at0, at1, at2, at3 = quarter == 0, quarter == 1, quarter == 2, quarter == 3
        free = jnp.where(near_low == (y == 0), 1, 2)
        early = jnp.logical_and(t == 1, at3)
        middling = jnp.logical_and(t == 2, quarter == free)
        late = jnp.logical_and(t == 2, at3)
        first_low = jnp.where(y == 0, 0, 2)
        middling_low, late_low = jnp.where(y == 0, 2, 0), 1
        middling_high, late_high = ne - 2, ne - 1
        extra = jnp.where(
            near_low,
            jnp.where(early, first_low, jnp.where(late, late_low, middling_low)),
            jnp.where(jnp.logical_or(early, middling), middling_high, late_high),
        )
        valid_extra = jnp.where(
            near_low,
            jnp.logical_or(early, jnp.logical_or(middling, late)),
            jnp.logical_and(
                near_high,
                jnp.logical_or(late, jnp.where(y == 0, early, middling)),
            ),
        )
        valid_post = jnp.logical_and(
            jnp.logical_and(t >= 1, t <= slabs),
            jnp.logical_or(at0, jnp.logical_and(at1, valid_b)),
        )
        valid_pre = jnp.logical_and(jnp.logical_and(t >= 1, t < slabs), jnp.logical_and(at2, valid_pre))
        task = jnp.where(at0, post_a, jnp.where(at1, post_b, pre))
        task = jnp.where(valid_extra, extra, task)
        valid = jnp.logical_or(valid_extra, jnp.logical_or(valid_post, valid_pre))
        valid = jnp.logical_and(on_quarter, valid)

        held = jnp.logical_or(t == slabs, jnp.logical_and(valid_pre, t == slabs - 1))
        paired = jnp.logical_and(valid_post, valid_b)

        @pl.when(jnp.logical_and(valid, jnp.logical_not(held)))
        def _():
            second = jnp.logical_and(paired, at1).astype(jnp.int32)
            whiten_into(task, part(wl, second), part(wr, second))

            @pl.when(jnp.logical_not(paired))
            def _():
                add(1)

            @pl.when(jnp.logical_and(paired, at1))
            def _():
                add(2)

        @pl.when(jnp.logical_and(valid, held))
        def _():
            whiten_into(task, part(wl_last, quarter), part(wr_last, quarter))

        return carry

    lax.fori_loop(0, nz * G + G // 4 + 1, step, 0)

    def drain(b, carry):
        def sent(buf, sem, part=rows):
            span = buf.at[b, pl.ds(0, part)]
            pltpu.make_async_copy(span, span, sem).wait()

        mine = b % 2 == y
        whole_b = jnp.logical_and(end, b == e + 1 - 2 * y)
        half_b = jnp.logical_and(near, b == 2 * far + 1 - y)

        @pl.when(jnp.logical_or(jnp.logical_and(mine, jnp.logical_and(has_up, b <= e)), jnp.logical_and(low, whole_b)))
        def _():
            sent(left, up_send.at[b])

        @pl.when(jnp.logical_or(jnp.logical_and(mine, jnp.logical_and(has_dn, b >= e)), jnp.logical_and(high, whole_b)))
        def _():
            sent(left, dn_send.at[b])

        @pl.when(jnp.logical_and(near_high, half_b))
        def _():
            sent(left, up_send.at[b], rows // 2)

        @pl.when(jnp.logical_and(near_low, half_b))
        def _():
            sent(left, dn_send.at[b], rows // 2)

        halved = jnp.logical_and(end, b == 2 * far + y)
        skipped = jnp.logical_and(near, b == 2 * beside + y)

        @pl.when(jnp.logical_and(mine, jnp.logical_not(jnp.logical_or(halved, skipped))))
        def _():
            sent(left, y_send.at[b])

        @pl.when(halved)
        def _():
            sent(left, y_send.at[b], rows // 2)

        @pl.when(is_src)
        def _():
            for i in range(1, nh):
                sent(right, x_send.at[b, i - 1])

        @pl.when(jnp.logical_or(is_src, is_relay))
        def _():
            sent(right, sib_send.at[b])

        return carry

    lax.fori_loop(0, ne, drain, 0)


def finish(tile, scale, gram_ref, wl_ref, wr_ref, out_ref, buf, sem):
    tiles = gram_ref.shape[0] // tile

    def write(i):
        cols = pl.ds(pl.multiple_of(i * tile, tile), tile)
        return pltpu.make_async_copy(buf.at[cols], out_ref.at[cols], sem.at[i])

    @pl.loop(0, tiles)
    def _(i):
        cols = pl.ds(pl.multiple_of(i * tile, tile), tile)
        product = lax.dot_general(
            wl_ref[:, cols], wr_ref[...], (((0,), (0,)), ((), ())), preferred_element_type=jnp.float32
        )
        buf[cols, :] = (gram_ref[cols, :] + product) * scale
        write(i).start()

    @pl.loop(0, tiles)
    def _(i):
        write(i).wait()


def on_device(ne, nc, partials, gaps, arc_start, taps):
    rows, width = partials.shape
    rwidth = width * nc // ne
    lags = jnp.pad(taps.astype(jnp.float32), (rows, rows - taps.shape[0]))[None, :]
    hbm, vmem = pl.BlockSpec(memory_space=pl.ANY), pl.BlockSpec(memory_space=pltpu.VMEM)
    gram, wl_last, wr_last = pl.pallas_call(
        functools.partial(kernel, ne, nc),
        out_shape=(
            pltpu.VMEM((width, rwidth), jnp.float32),
            pltpu.VMEM((3 * rows, width), jnp.bfloat16),
            pltpu.VMEM((3 * rows, rwidth), jnp.bfloat16),
        ),
        in_specs=[pl.BlockSpec(memory_space=pltpu.SMEM), hbm, hbm, hbm],
        out_specs=(vmem, vmem, vmem),
        scratch_shapes=[
            pltpu.VMEM((ne + 1, rows, width), jnp.bfloat16),
            pltpu.VMEM((ne + 1, rows, rwidth), jnp.bfloat16),
            pltpu.VMEM((rows, 2 * rows), jnp.float32),
            pltpu.VMEM((2 * rows, width), jnp.bfloat16),
            pltpu.VMEM((2 * rows, rwidth), jnp.bfloat16),
            pltpu.VMEM((1, rows), jnp.int32),
            pltpu.VMEM((1, 2 * rows), jnp.float32),
            pltpu.SemaphoreType.DMA((ne, CHUNKS)),
            pltpu.SemaphoreType.DMA((ne, CHUNKS)),
            pltpu.SemaphoreType.DMA((ne,)),
            pltpu.SemaphoreType.DMA((ne,)),
            pltpu.SemaphoreType.DMA((ne,)),
            pltpu.SemaphoreType.DMA((ne,)),
            pltpu.SemaphoreType.DMA((ne, nc // 2)),
            pltpu.SemaphoreType.DMA((3,)),
        ],
        compiler_params=pltpu.CompilerParams(
            collective_id=0, has_side_effects=True, vmem_limit_bytes=44 * 1024 * 1024
        ),
        cost_estimate=pl.CostEstimate(
            flops=2 * ne * rows * width * rwidth, bytes_accessed=4 * width * rwidth, transcendentals=0
        ),
    )(arc_start, gaps[None, :], lags, partials)
    tile = min(256, width)
    return pl.pallas_call(
        functools.partial(finish, tile, (rows * ne) ** (-0.5)),
        out_shape=jax.ShapeDtypeStruct((width, rwidth), jnp.float32),
        in_specs=[vmem, vmem, vmem],
        out_specs=hbm,
        scratch_shapes=[
            pltpu.VMEM((width, rwidth), jnp.float32),
            pltpu.SemaphoreType.DMA((width // tile,)),
        ],
        compiler_params=pltpu.CompilerParams(vmem_limit_bytes=24 * 1024 * 1024),
        cost_estimate=pl.CostEstimate(
            flops=4 * rows * width * rwidth, bytes_accessed=4 * width * rwidth, transcendentals=0
        ),
    )(gram, wl_last, wr_last)


def solution(mesh):
    in_specs = (P("epoch", "col"), P("epoch"), P(), P())
    out_specs = P("col", "epoch")
    ne, nc = mesh.shape["epoch"], mesh.shape["col"]
    return jax.shard_map(
        functools.partial(on_device, ne, nc),
        mesh=mesh, in_specs=in_specs, out_specs=out_specs, check_vma=False,
    )
```

```python
import functools

import jax
import jax.numpy as jnp
from jax import lax
from jax.experimental import pallas as pl
from jax.experimental.pallas import tpu as pltpu
from jax.sharding import PartitionSpec as P

MESH = pl.DeviceIdType.MESH
CHUNKS = 8


def kernel(
    ne, nc, arc_ref, gaps_ref, taps_ref, part_ref, out_ref, wl_last, wr_last,
    left_all, right_all, table, wl, wr, gaps_here, taps_here,
    left_recv, right_recv, up_send, dn_send, y_send, sib_send, x_send, in_sem,
):
    rows, width = part_ref.shape
    rwidth = right_all.shape[2]
    nz, nh = ne // 2, nc // 2
    left, right = left_all.at[pl.ds(1, ne)], right_all.at[pl.ds(1, ne)]
    G = CHUNKS
    crows = rows // G
    e, c = lax.axis_index("epoch"), lax.axis_index("col")
    z, y = e // 2, e % 2
    h, k = c // 2, c % 2
    src = e * nc // ne
    h_src, k_src = src // 2, src % 2
    offset = pl.multiple_of((e * nc % ne) // nc * rwidth, rwidth)
    is_src = c == src
    is_relay = jnp.logical_and(k == k_src, h != h_src)
    has_up, has_dn = z < nz - 1, z > 0
    up, dn, across, sib = e + 2, e - 2, e + 1 - 2 * y, c + 1 - 2 * k

    low, high = z == 0, z == nz - 1
    near_low, near_high = z == 1, z == nz - 2
    end, near = jnp.logical_or(low, high), jnp.logical_or(near_low, near_high)
    slabs = jnp.where(near, nz - 1, nz)
    far = jnp.where(z <= 1, nz - 1, 0)
    beside = jnp.where(z <= 1, 0, nz - 1)

    load_rows = pltpu.make_async_copy(part_ref, left.at[e], in_sem.at[0])
    load_gaps = pltpu.make_async_copy(gaps_ref, gaps_here, in_sem.at[1])
    load_taps = pltpu.make_async_copy(taps_ref, taps_here, in_sem.at[2])
    load_rows.start()
    load_gaps.start()
    load_taps.start()
    barrier = pltpu.get_barrier_semaphore()

    def greet(ee, cc):
        pl.semaphore_signal(barrier, inc=1, device_id=(ee, cc), device_id_type=MESH)

    @pl.when(has_up)
    def _():
        greet(up, c)

    @pl.when(has_dn)
    def _():
        greet(dn, c)

    greet(across, c)
    for i in range(1, nc):
        greet(e, lax.rem(c + i, nc))

    load_rows.wait()
    load_gaps.wait()
    load_taps.wait()
    eye = lax.broadcasted_iota(jnp.int32, (rows, rows), 0) == lax.broadcasted_iota(jnp.int32, (rows, rows), 1)
    column = jnp.sum(jnp.where(eye, gaps_here[...].astype(jnp.float32), 0.0), axis=1, keepdims=True)
    left[e] = left[e] * column.astype(jnp.bfloat16)

    pl.semaphore_wait(barrier, nc + has_up.astype(jnp.int32) + has_dn.astype(jnp.int32))

    def slab(t):
        both = 2 * jnp.minimum(z, nz - 1 - z)
        alternate = jnp.where(t % 2 == 1, z - (t + 1) // 2, z + t // 2)
        rest = jnp.where(z <= nz - 1 - z, t, nz - 1 - t)
        middle = jnp.where(t <= both, alternate, rest)
        return jnp.where(z <= 1, z + t, jnp.where(z >= nz - 2, z - t, middle))

    b_last = 2 * slab(slabs - 1) + 1 - y

    def piece(buf, b, g):
        return buf.at[b, pl.ds(pl.multiple_of(g * crows, crows), crows)]

    halves = 2 * rwidth == width
    groups = G // 4

    def last_rows(i):
        if not halves:
            return pl.ds(pl.multiple_of(i * crows, crows), crows)
        group = i // (G // 2) * groups + i % groups
        return pl.ds(pl.multiple_of(group * 2 * crows, 2 * crows), 2 * crows)

    def last_piece(b, i, ee):
        if not halves:
            return left.at[b, last_rows(i)]
        second = (i % (G // 2) // groups + ee * nc % ne // nc) % 2
        return left.at[b, last_rows(i), pl.ds(pl.multiple_of(second * rwidth, rwidth), rwidth)]

    def last_spreads(i):
        return i % (G // 2) < groups if halves else i >= 0

    def send_last(b, i, sem, ee):
        pltpu.make_async_remote_copy(
            src_ref=last_piece(b, i, ee), dst_ref=last_piece(b, i, ee),
            send_sem=sem.at[b], recv_sem=left_recv.at[b, i],
            device_id=(ee, c), device_id_type=MESH,
        ).start()

    def spread_last(b, i):
        source = left.at[b, last_rows(i), pl.ds(offset, rwidth)]
        target = right.at[b, last_rows(i)]

        def send(sem, cc):
            pltpu.make_async_remote_copy(
                src_ref=source, dst_ref=target, send_sem=sem, recv_sem=right_recv.at[b, i],
                device_id=(e, cc), device_id_type=MESH,
            ).start()

        @pl.when(jnp.logical_and(is_src, last_spreads(i)))
        def _():
            for n in range(1, nh):
                send(x_send.at[b, n - 1], lax.rem(h + n, nh) * 2 + k)
            send(sib_send.at[b], sib)
            pltpu.make_async_copy(source, target, right_recv.at[b, i]).start()

    def send_left(b, g, sem, ee):
        pltpu.make_async_remote_copy(
            src_ref=piece(left, b, g), dst_ref=piece(left, b, g),
            send_sem=sem.at[b], recv_sem=left_recv.at[b, g],
            device_id=(ee, c), device_id_type=MESH,
        ).start()

    def right_source(b, g):
        return left.at[b, pl.ds(pl.multiple_of(g * crows, crows), crows), pl.ds(offset, rwidth)]

    def send_right(source, b, g, sem, cc):
        pltpu.make_async_remote_copy(
            src_ref=source, dst_ref=piece(right, b, g),
            send_sem=sem, recv_sem=right_recv.at[b, g],
            device_id=(e, cc), device_id_type=MESH,
        ).start()

    def spread(b, g):
        @pl.when(is_src)
        def _():
            for i in range(1, nh):
                send_right(right_source(b, g), b, g, x_send.at[b, i - 1], lax.rem(h + i, nh) * 2 + k)
            send_right(right_source(b, g), b, g, sib_send.at[b], sib)
            pltpu.make_async_copy(right_source(b, g), piece(right, b, g), right_recv.at[b, g]).start()

    def wait_left(b, g):
        pltpu.make_async_copy(piece(left, b, g), piece(left, b, g), left_recv.at[b, g]).wait()

    def wait_right(b, g):
        pltpu.make_async_copy(piece(right, b, g), piece(right, b, g), right_recv.at[b, g]).wait()

        @pl.when(is_relay)
        def _():
            send_right(piece(right, b, g), b, g, sib_send.at[b], sib)

    def own(g, carry):
        @pl.when(has_up)
        def _():
            send_left(e, g, up_send, up)

        @pl.when(has_dn)
        def _():
            send_left(e, g, dn_send, dn)

        send_left(e, g, y_send, across)
        spread(e, g)
        return carry

    lax.fori_loop(0, G, own, 0)

    lags = pltpu.roll(
        jnp.broadcast_to(taps_here[...], (2 * rows, 2 * rows)), 0, 1, stride=1, stride_axis=0
    )
    table[...] = lags[:, :rows].T
    left_all[0] = jnp.zeros((rows, width), jnp.bfloat16)
    right_all[0] = jnp.zeros((rows, rwidth), jnp.bfloat16)
    out_ref[...] = jnp.zeros_like(out_ref)
    wl_last[rows:] = jnp.zeros((2 * rows, width), jnp.bfloat16)
    wr_last[rows:] = jnp.zeros((2 * rows, rwidth), jnp.bfloat16)

    def whiten_into(b, into_left, into_right):
        first = b * rows
        later = first + lax.broadcasted_iota(jnp.int32, (rows, 2 * rows), 0)
        source = first - rows + lax.broadcasted_iota(jnp.int32, (rows, 2 * rows), 1)
        boundary = arc_ref[0]
        same = (later >= boundary) == (source >= boundary)
        keep = jnp.logical_and(same, source >= 0)
        taps = jnp.where(keep, table[...], 0.0).astype(jnp.bfloat16)

        def whiten(buf, into, step):
            @pl.loop(0, into.shape[1] // step)
            def _(i):
                cols = pl.ds(pl.multiple_of(i * step, step), step)
                both = buf[pl.ds(b, 2), :, cols].reshape(2 * rows, step)
                white = jnp.dot(taps, both, preferred_element_type=jnp.float32)
                into[:, cols] = white.astype(jnp.bfloat16)

        whiten(left_all, into_left, min(512, width))
        whiten(right_all, into_right, min(512, rwidth))

    def add(blocks):
        depth = pl.ds(0, blocks * rows)

        @pl.loop(0, width // 256)
        def _(i):
            cols = pl.ds(pl.multiple_of(i * 256, 256), 256)
            out_ref[cols, :] += lax.dot_general(
                wl[depth, cols], wr[depth, :], (((0,), (0,)), ((), ())), preferred_element_type=jnp.float32
            )

    def part(buf, i):
        return buf.at[pl.ds(pl.multiple_of(i * rows, rows), rows)]

    def chunk(t, g):
        side = g % 2 * (G // 2) + g // 2
        turned = (g + G // 2) % G
        ends_last = jnp.logical_and(end, t == nz - 1)
        return jnp.where(ends_last, side, jnp.where(jnp.logical_and(near, t == nz - 2), turned, g))

    def step(it, carry):
        t, g = it // G, it % G
        moving = t < nz

        @pl.when(t == 0)
        def _():
            wait_right(e, g)

        last = jnp.maximum(it - 1, 0)
        pt, pg = last // G, last % G
        passed = jnp.logical_and(it >= 1, pt < nz)

        @pl.when(jnp.logical_and(passed, z - pt - 1 >= 0))
        def _():
            wait_right(e - 2 * (pt + 1), pg)

        @pl.when(jnp.logical_and(passed, z + pt + 1 < nz))
        def _():
            wait_right(e + 2 * (pt + 1), pg)

        ends_past = jnp.logical_and(end, pt == nz - 1)

        @pl.when(jnp.logical_and(it >= 1, jnp.logical_and(pt < slabs, jnp.logical_not(ends_past))))
        def _():
            wait_right(2 * slab(pt) + 1 - y, chunk(pt, pg))

        @pl.when(jnp.logical_and(ends_past, last_spreads(chunk(pt, pg))))
        def _():
            i = chunk(pt, pg)
            rows_here = right.at[b_last, last_rows(i)]
            pltpu.make_async_copy(rows_here, rows_here, right_recv.at[b_last, i]).wait()

            @pl.when(is_relay)
            def _():
                pltpu.make_async_remote_copy(
                    src_ref=rows_here, dst_ref=rows_here,
                    send_sem=sib_send.at[b_last], recv_sem=right_recv.at[b_last, i],
                    device_id=(e, sib), device_id_type=MESH,
                ).start()

        @pl.when(jnp.logical_and(it >= 1, jnp.logical_and(near, pt == 1)))
        def _():
            wait_right(2 * beside + 1 - y, pg)

        @pl.when(jnp.logical_and(moving, z - t - 1 >= 0))
        def _():
            b = e - 2 * (t + 1)
            wait_left(b, g)

            @pl.when(has_up)
            def _():
                send_left(b, g, up_send, up)

            spread(b, g)

        @pl.when(jnp.logical_and(moving, z + t + 1 < nz))
        def _():
            b = e + 2 * (t + 1)
            wait_left(b, g)

            @pl.when(has_dn)
            def _():
                send_left(b, g, dn_send, dn)

            spread(b, g)

        half = G // 2
        ends_next = jnp.logical_and(end, t + 1 == nz - 1)
        near_next = jnp.logical_and(near, t + 1 == nz - 2)
        near_last = jnp.logical_and(near, t == nz - 2)

        @pl.when(jnp.logical_or(
            jnp.logical_and(
                t + 1 < slabs,
                jnp.logical_not(jnp.logical_or(ends_next, jnp.logical_and(near_next, g < half))),
            ),
            jnp.logical_and(near_last, g < half),
        ))
        def _():
            send_left(2 * slab(jnp.minimum(t + 1, slabs - 1)) + y, g, y_send, across)

        @pl.when(jnp.logical_and(ends_next, g == half - 1))
        def _():
            for i in range(half):
                send_last(2 * far + y, i, y_send, across)

        ends_last = jnp.logical_and(end, t == nz - 1)

        @pl.when(ends_last)
        def _():
            i = chunk(t, g)
            piece_here = last_piece(b_last, i, e)
            pltpu.make_async_copy(piece_here, piece_here, left_recv.at[b_last, i]).wait()
            spread_last(b_last, i)

        @pl.when(jnp.logical_and(t < slabs, jnp.logical_not(ends_last)))
        def _():
            b = 2 * slab(t) + 1 - y
            wait_left(b, chunk(t, g))
            to_near = jnp.logical_and(end, t == 0)
            to_end = jnp.logical_and(near_last, g == half - 1)

            @pl.when(jnp.logical_and(low, to_near))
            def _():
                send_left(b, g, up_send, up)

            @pl.when(jnp.logical_and(high, to_near))
            def _():
                send_left(b, g, dn_send, dn)

            @pl.when(jnp.logical_and(near_high, to_end))
            def _():
                for i in range(half, G):
                    send_last(b, i, up_send, up)

            @pl.when(jnp.logical_and(near_low, to_end))
            def _():
                for i in range(half, G):
                    send_last(b, i, dn_send, dn)

            spread(b, chunk(t, g))

        @pl.when(jnp.logical_and(near, t == 1))
        def _():
            b = 2 * beside + 1 - y
            wait_left(b, g)
            spread(b, g)

        s = slab(jnp.clip(t - 1, 0, slabs - 1))
        s_now = slab(jnp.minimum(t, slabs - 1))
        below = s < z
        post_a = jnp.where(s > z, 2 * s + 1 - y, 2 * s + 1)
        post_b = jnp.where(
            s > z,
            2 * s + 1,
            jnp.where(jnp.logical_and(below, y == 0), 2 * s + 2, 0),
        )
        valid_b = jnp.where(
            s > z,
            y == 1,
            jnp.where(below, jnp.logical_or(y == 0, s == 0), s == 0),
        )
        pre = jnp.where(s_now > z, 2 * s_now, jnp.where(y == 0, 0, 2 * s_now + 2))
        valid_pre = jnp.where(
            s_now > z, y == 0, jnp.logical_and(s_now < z, jnp.logical_or(y == 1, s_now == 0))
        )
        quarter, on_quarter = g // (G // 4), g % (G // 4) == 0
        at0, at1, at2, at3 = quarter == 0, quarter == 1, quarter == 2, quarter == 3
        free = jnp.where(near_low == (y == 0), 1, 2)
        early = jnp.logical_and(t == 1, at3)
        middling = jnp.logical_and(t == 2, quarter == free)
        late = jnp.logical_and(t == 2, at3)
        first_low = jnp.where(y == 0, 0, 2)
        middling_low, late_low = jnp.where(y == 0, 2, 0), 1
        middling_high, late_high = ne - 2, ne - 1
        extra = jnp.where(
            near_low,
            jnp.where(early, first_low, jnp.where(late, late_low, middling_low)),
            jnp.where(jnp.logical_or(early, middling), middling_high, late_high),
        )
        valid_extra = jnp.where(
            near_low,
            jnp.logical_or(early, jnp.logical_or(middling, late)),
            jnp.logical_and(
                near_high,
                jnp.logical_or(late, jnp.where(y == 0, early, middling)),
            ),
        )
        valid_post = jnp.logical_and(
            jnp.logical_and(t >= 1, t <= slabs),
            jnp.logical_or(at0, jnp.logical_and(at1, valid_b)),
        )
        valid_pre = jnp.logical_and(jnp.logical_and(t >= 1, t < slabs), jnp.logical_and(at2, valid_pre))
        task = jnp.where(at0, post_a, jnp.where(at1, post_b, pre))
        task = jnp.where(valid_extra, extra, task)
        valid = jnp.logical_or(valid_extra, jnp.logical_or(valid_post, valid_pre))
        valid = jnp.logical_and(on_quarter, valid)

        held = jnp.logical_or(t == slabs, jnp.logical_and(valid_pre, t == slabs - 1))
        paired = jnp.logical_and(valid_post, valid_b)

        @pl.when(jnp.logical_and(valid, jnp.logical_not(held)))
        def _():
            second = jnp.logical_and(paired, at1).astype(jnp.int32)
            whiten_into(task, part(wl, second), part(wr, second))

            @pl.when(jnp.logical_not(paired))
            def _():
                add(1)

            @pl.when(jnp.logical_and(paired, at1))
            def _():
                add(2)

        @pl.when(jnp.logical_and(valid, held))
        def _():
            whiten_into(task, part(wl_last, quarter), part(wr_last, quarter))

        return carry

    lax.fori_loop(0, nz * G + G // 4 + 1, step, 0)

    def drain(b, carry):
        def sent(buf, sem, part=rows):
            span = buf.at[b, pl.ds(0, part)]
            pltpu.make_async_copy(span, span, sem).wait()

        mine = b % 2 == y
        whole_b = jnp.logical_and(end, b == e + 1 - 2 * y)
        half_b = jnp.logical_and(near, b == 2 * far + 1 - y)

        @pl.when(jnp.logical_or(jnp.logical_and(mine, jnp.logical_and(has_up, b <= e)), jnp.logical_and(low, whole_b)))
        def _():
            sent(left, up_send.at[b])

        @pl.when(jnp.logical_or(jnp.logical_and(mine, jnp.logical_and(has_dn, b >= e)), jnp.logical_and(high, whole_b)))
        def _():
            sent(left, dn_send.at[b])

        @pl.when(jnp.logical_and(near_high, half_b))
        def _():
            sent(left, up_send.at[b], rows // 2)

        @pl.when(jnp.logical_and(near_low, half_b))
        def _():
            sent(left, dn_send.at[b], rows // 2)

        halved = jnp.logical_and(end, b == 2 * far + y)
        skipped = jnp.logical_and(near, b == 2 * beside + y)

        @pl.when(jnp.logical_and(mine, jnp.logical_not(jnp.logical_or(halved, skipped))))
        def _():
            sent(left, y_send.at[b])

        @pl.when(halved)
        def _():
            sent(left, y_send.at[b], rows // 2)

        @pl.when(is_src)
        def _():
            for i in range(1, nh):
                sent(right, x_send.at[b, i - 1])

        @pl.when(jnp.logical_or(is_src, is_relay))
        def _():
            sent(right, sib_send.at[b])

        return carry

    lax.fori_loop(0, ne, drain, 0)


def finish(tile, scale, gram_ref, wl_ref, wr_ref, out_ref, buf, sem):
    tiles = gram_ref.shape[0] // tile

    def write(i):
        cols = pl.ds(pl.multiple_of(i * tile, tile), tile)
        return pltpu.make_async_copy(buf.at[cols], out_ref.at[cols], sem.at[i])

    @pl.loop(0, tiles)
    def _(i):
        cols = pl.ds(pl.multiple_of(i * tile, tile), tile)
        product = lax.dot_general(
            wl_ref[:, cols], wr_ref[...], (((0,), (0,)), ((), ())), preferred_element_type=jnp.float32
        )
        buf[cols, :] = (gram_ref[cols, :] + product) * scale
        write(i).start()

    @pl.loop(0, tiles)
    def _(i):
        write(i).wait()


def on_device(ne, nc, partials, gaps, arc_start, taps):
    rows, width = partials.shape
    rwidth = width * nc // ne
    lags = jnp.pad(taps.astype(jnp.float32), (rows, rows - taps.shape[0]))[None, :]
    hbm, vmem = pl.BlockSpec(memory_space=pl.ANY), pl.BlockSpec(memory_space=pltpu.VMEM)
    gram, wl_last, wr_last = pl.pallas_call(
        functools.partial(kernel, ne, nc),
        out_shape=(
            pltpu.VMEM((width, rwidth), jnp.float32),
            pltpu.VMEM((3 * rows, width), jnp.bfloat16),
            pltpu.VMEM((3 * rows, rwidth), jnp.bfloat16),
        ),
        in_specs=[pl.BlockSpec(memory_space=pltpu.SMEM), hbm, hbm, hbm],
        out_specs=(vmem, vmem, vmem),
        scratch_shapes=[
            pltpu.VMEM((ne + 1, rows, width), jnp.bfloat16),
            pltpu.VMEM((ne + 1, rows, rwidth), jnp.bfloat16),
            pltpu.VMEM((rows, 2 * rows), jnp.float32),
            pltpu.VMEM((2 * rows, width), jnp.bfloat16),
            pltpu.VMEM((2 * rows, rwidth), jnp.bfloat16),
            pltpu.VMEM((1, rows), jnp.int32),
            pltpu.VMEM((1, 2 * rows), jnp.float32),
            pltpu.SemaphoreType.DMA((ne, CHUNKS)),
            pltpu.SemaphoreType.DMA((ne, CHUNKS)),
            pltpu.SemaphoreType.DMA((ne,)),
            pltpu.SemaphoreType.DMA((ne,)),
            pltpu.SemaphoreType.DMA((ne,)),
            pltpu.SemaphoreType.DMA((ne,)),
            pltpu.SemaphoreType.DMA((ne, nc // 2)),
            pltpu.SemaphoreType.DMA((3,)),
        ],
        compiler_params=pltpu.CompilerParams(
            collective_id=0, has_side_effects=True, vmem_limit_bytes=44 * 1024 * 1024
        ),
        cost_estimate=pl.CostEstimate(
            flops=2 * ne * rows * width * rwidth, bytes_accessed=4 * width * rwidth, transcendentals=0
        ),
    )(arc_start, gaps[None, :], lags, partials)
    tile = min(256, width)
    return pl.pallas_call(
        functools.partial(finish, tile, (rows * ne) ** (-0.5)),
        out_shape=jax.ShapeDtypeStruct((width, rwidth), jnp.float32),
        in_specs=[vmem, vmem, vmem],
        out_specs=hbm,
        scratch_shapes=[
            pltpu.VMEM((width, rwidth), jnp.float32),
            pltpu.SemaphoreType.DMA((width // tile,)),
        ],
        compiler_params=pltpu.CompilerParams(vmem_limit_bytes=24 * 1024 * 1024),
        cost_estimate=pl.CostEstimate(
            flops=4 * rows * width * rwidth, bytes_accessed=4 * width * rwidth, transcendentals=0
        ),
    )(gram, wl_last, wr_last)


def solution(mesh):
    in_specs = (P("epoch", "col"), P("epoch"), P(), P())
    out_specs = P("col", "epoch")
    ne, nc = mesh.shape["epoch"], mesh.shape["col"]
    return jax.shard_map(
        functools.partial(on_device, ne, nc),
        mesh=mesh, in_specs=in_specs, out_specs=out_specs, check_vma=False,
    )
```
